32 devices in a mesh: layer: 8 (over z, y), lat: 4 (over x, core).
Axes of the slice: x: 2, y: 2, z: 4, core: 2. Of those that a mesh axis runs over, the one named last changes fastest.
Arguments:
- inputs: bfloat16 [128, 2, 2048], P(None, None, 'layer'), may hold values from -6 to 6
- encoder: bfloat16 [2, 2048, 4096], P(None, 'layer', 'lat'), may hold values from -0.125 to 0.125
- enc_bias: float32 [2, 4096], P(None, 'lat'), may hold values from -3 to 3
- decoder: bfloat16 [8, 3, 4096, 256], P('layer', None, 'lat'), may hold values from -0.5 to 0.5
- dec_bias: float32 [8, 2, 256], P('layer'), may hold values from -3 to 3
- targets: bfloat16 [8, 128, 2, 256], P('layer'), may hold values from -6 to 6
- top_index: int32 [128, 2, 64], replicated, may hold values from 0 to 4095, as said below
Outputs:
- decoder_grad: float32 [8, 3, 4096, 256], P('layer', None, 'lat')
- encoder_grad: float32 [2, 2048, 4096], P(None, 'layer', 'lat')
- bias_grad: float32 [2, 4096], P(None, 'lat')
The draws below stay inside these ranges and needn't reach their ends.
Inputs may be any that keep to these rules, and one draw needn't show every extreme that they name: `top_index`: the 64 entries of one token and layer are distinct; at most 32 of them have the same value of n // 1024, and every value of n // 1024 is taken by exactly 32 entries of some token and layer.
All inputs are finite; a program needn't handle non-finite values.
Results may differ from the reference program's by a relative error of at most 0.0045.
Values may be sent and summed in bfloat16 or wider, within the bound.
No kernel may reach another device: no remote copies, remote signals or barrier semaphores. Data moves between devices by JAX's collectives and lax.ppermute only.
A program may use at most 64 MiB of HBM per device.

```python
import jax
import jax.numpy as jnp
from jax import lax

D = 2048
LAT_DEV = 1024
LATENTS = 4096
TOKENS = 128
TOPK = 64
SLAB_MOST = 32
FEAT_SPLIT = 8
FEAT_BLK = 256
LAYERS = 2
N_LAYER = 8


def draw_top_index(key, part):
    group_count = LATENTS // LAT_DEV
    cell_count = group_count * SLAB_MOST
    row_count = TOKENS * LAYERS
    key_list = jax.random.split(jax.random.fold_in(key, 7101), 5)
    offset = jax.random.randint(key_list[0], (), 0, group_count)
    full_group = (jnp.arange(row_count, dtype=jnp.int32) + offset) % group_count
    cell_ids = jnp.arange(cell_count, dtype=jnp.int32)
    cell_group = cell_ids // SLAB_MOST
    scores = jax.random.randint(key_list[1], (row_count, cell_count), 0, 2 ** 20)
    scores = scores + jnp.where(cell_group[None, :] == full_group[:, None], 2 ** 21, 0)
    scores = scores * cell_count + cell_ids[None, :]
    unused, chosen = lax.top_k(scores, TOPK)
    order_key = jax.random.randint(key_list[2], (row_count, TOPK), 0, 2 ** 20) * TOPK + jnp.arange(TOPK, dtype=jnp.int32)[None, :]
    ordering = jnp.argsort(order_key, axis=1)
    chosen = jnp.take_along_axis(chosen, ordering, axis=1)
    chosen_group = chosen // SLAB_MOST
    chosen_rank = chosen % SLAB_MOST
    base_offset = jax.random.randint(key_list[3], (row_count, group_count), 0, LAT_DEV)
    stride = 2 * jax.random.randint(key_list[4], (row_count, group_count), 0, LAT_DEV // 2) + 1
    group_base = jnp.take_along_axis(base_offset, chosen_group, axis=1)
    group_stride = jnp.take_along_axis(stride, chosen_group, axis=1)
    latent = chosen_group * LAT_DEV + (group_base + chosen_rank * group_stride) % LAT_DEV
    return latent.reshape(TOKENS, LAYERS, TOPK).astype(jnp.int32)


def levels(stream_key, extent, pieces, least, high):
    level = 1.0
    for position, parts in pieces:
        steps = jax.random.uniform(jax.random.fold_in(jax.random.fold_in(stream_key, 6), position), (parts,), jnp.float32, least / len(pieces), high / len(pieces))
        level = level * jnp.repeat(jnp.exp(steps), extent[position] // parts).reshape((-1,) + (1,) * (len(extent) - 1 - position))
    return level


def gaussian(key, extent, scale, most, pieces=(), held_as=jnp.bfloat16):
    array = jax.random.normal(key, extent, jnp.float32) * scale
    if len(pieces) > 0:
        array = levels(key, extent, pieces, -0.22, 0.18) * array
    return jnp.clip(array, min=-most, max=most).astype(held_as)


def setup_inputs(seed: int = 0) -> dict:
    streams_of = jax.random.split(jax.random.key(seed), 8)
    return {
        "inputs": gaussian(streams_of[0], (TOKENS, LAYERS, D), 1.0, 6.0, ((2, 8),)),
        "encoder": gaussian(streams_of[1], (LAYERS, D, LATENTS), D ** -0.5, 0.125, ((1, 8), (2, 4))),
        "enc_bias": gaussian(streams_of[2], (LAYERS, LATENTS), 0.5, 3.0, ((1, 4),), jnp.float32),
        "decoder": gaussian(streams_of[3], (N_LAYER, LAYERS + 1, LATENTS, FEAT_BLK), (TOPK * LAYERS) ** -0.5, 0.5, ((0, 8), (2, 4))),
        "dec_bias": gaussian(streams_of[4], (N_LAYER, 2, FEAT_BLK), 0.5, 3.0, ((0, 8),), jnp.float32),
        "targets": gaussian(streams_of[5], (N_LAYER, TOKENS, 2, FEAT_BLK), 1.0, 6.0, ((0, 8),)),
        "top_index": draw_top_index(jax.random.fold_in(streams_of[7], 71), 0),
    }


def reference(inputs, encoder, enc_bias, decoder, dec_bias, targets, top_index):
    pre_values = []
    for layer_id in range(LAYERS):
        picked = top_index[:, layer_id, :]
        columns = jnp.take(encoder[layer_id].T, picked, axis=0)
        values = jnp.einsum("td,tkd->tk", inputs[:, layer_id, :].astype(jnp.float32), columns.astype(jnp.float32))
        values = values + jnp.take(enc_bias[layer_id], picked, axis=0)
        pre_values.append(lax.optimization_barrier(values.astype(jnp.bfloat16)))
    grad_values = [jnp.zeros((TOKENS, TOPK), jnp.float32) for layer_id in range(LAYERS)]
    decoder_rows = []
    for row_index in range(N_LAYER):
        pair_index = row_index // FEAT_SPLIT
        block_plan = []
        for block_index in range(LAYERS + 1):
            if block_index <= pair_index:
                block_plan.append((block_index, block_index, 0))
            else:
                block_plan.append((block_index, block_index - pair_index - 1, 1))
        gathered = {}
        slot_sums = [dec_bias[row_index, 0][None, :] + jnp.zeros((TOKENS, FEAT_BLK), jnp.float32),
                     dec_bias[row_index, 1][None, :] + jnp.zeros((TOKENS, FEAT_BLK), jnp.float32)]
        for block_index, source, slot_index in block_plan:
            row_weights = jnp.take(decoder[row_index, block_index], top_index[:, source, :], axis=0).astype(jnp.float32)
            gathered[block_index] = row_weights
            slot_sums[slot_index] = slot_sums[slot_index] + jnp.einsum("tk,tkf->tf", pre_values[source].astype(jnp.float32), row_weights)
        residues = []
        for slot_index in range(2):
            residue = slot_sums[slot_index] - targets[row_index, :, slot_index, :].astype(jnp.float32)
            residues.append(lax.optimization_barrier(residue.astype(jnp.bfloat16)))
        block_grads = []
        for block_index, source, slot_index in block_plan:
            residue = residues[slot_index].astype(jnp.float32)
            updates = pre_values[source].astype(jnp.float32)[:, :, None] * residue[:, None, :]
            block_grad = jnp.zeros((LATENTS, FEAT_BLK), jnp.float32).at[top_index[:, source, :]].add(updates)
            block_grads.append(block_grad)
            grad_values[source] = grad_values[source] + jnp.einsum("tf,tkf->tk", residue, gathered[block_index])
        decoder_rows.append(jnp.stack(block_grads, axis=0))
    decoder_grad = jnp.stack(decoder_rows, axis=0)
    encoder_layers = []
    bias_layers = []
    for layer_id in range(LAYERS):
        picked = top_index[:, layer_id, :]
        pre_grad = lax.optimization_barrier(grad_values[layer_id].astype(jnp.bfloat16)).astype(jnp.float32)
        updates = pre_grad[:, :, None] * inputs[:, layer_id, :].astype(jnp.float32)[:, None, :]
        transposed = jnp.zeros((LATENTS, D), jnp.float32).at[picked].add(updates)
        encoder_layers.append(transposed.T)
        bias_layers.append(jnp.zeros((LATENTS,), jnp.float32).at[picked].add(pre_grad))
    return decoder_grad, jnp.stack(encoder_layers, axis=0), jnp.stack(bias_layers, axis=0)
```

```python
import functools

import jax
import jax.numpy as jnp
from jax import lax
from jax.experimental import pallas as pl
from jax.experimental.pallas import tpu as pltpu
from jax.sharding import PartitionSpec as P

FEAT_SPLIT = 8
LANES = 128
CELL = 256

BF = jnp.bfloat16
F32 = jnp.float32
NT = (((1,), (1,)), ((), ()))
TN = (((0,), (0,)), ((), ()))


def matmul(left, right, dims=(((1,), (0,)), ((), ()))):
    return lax.dot_general(left, right, dims, preferred_element_type=F32)


def flag(condition):
    return jnp.where(condition, 1.0, 0.0).astype(BF)


def iota(shape, dimension):
    return lax.broadcasted_iota(jnp.int32, shape, dimension)


def cell_masks(cell_index, rows):
    row = lax.shift_right_arithmetic(cell_index, 7)
    lane = jnp.bitwise_and(cell_index, LANES - 1)
    row_hit = iota((rows, CELL), 0) == row
    lane_hot = flag(iota((LANES, CELL), 0) == lane)
    return row_hit, lane_hot


def gather_slots(dense, zidx_ref, out_ref, layer, cells, tokens_cell, width):
    blocks = width // LANES
    for cell in range(cells):
        view = jnp.concatenate(
            [
                dense[cell * tokens_cell : (cell + 1) * tokens_cell, b * LANES : (b + 1) * LANES]
                for b in range(blocks)
            ],
            axis=0,
        ).astype(BF)
        at = layer * cells + cell
        row_hit, lane_hot = cell_masks(zidx_ref[at : at + 1, :], blocks * tokens_cell)
        spread = matmul(view, lane_hot)
        out_ref[at : at + 1, :] = jnp.sum(jnp.where(row_hit, spread, 0.0), axis=0, keepdims=True)


def scatter_slots(values, zidx_ref, dense_ref, layer, cells, tokens_cell, width):
    blocks = width // LANES
    group = max(1, 16 // tokens_cell)
    for first in range(0, cells, group):
        views = []
        for cell in range(first, first + group):
            at = layer * cells + cell
            row_hit, lane_hot = cell_masks(zidx_ref[at : at + 1, :], blocks * tokens_cell)
            placed = jnp.where(row_hit, values[at : at + 1, :], 0.0).astype(BF)
            views.append(matmul(placed, lane_hot, NT))
        for b in range(blocks):
            piece = [v[b * tokens_cell : (b + 1) * tokens_cell] for v in views]
            piece = piece[0] if group == 1 else jnp.concatenate(piece, axis=0)
            dense_ref[
                layer,
                first * tokens_cell : (first + group) * tokens_cell,
                b * LANES : (b + 1) * LANES,
            ] = piece.astype(BF)


def slot_index(top, slab, width, layers, top_count, slab_most, tokens_cell):
    tokens, lanes = top.shape
    cells = tokens // tokens_cell
    lane = iota(top.shape, 1)
    place = jnp.bitwise_and(lane, top_count - 1)
    local = top - slab * width
    inside = (local >= 0) & (local < width)
    before = iota((lanes, lanes), 0)
    after = iota((lanes, lanes), 1)
    earlier = flag((before // top_count == after // top_count) & (before < after))
    rank = matmul(flag(inside), earlier).astype(jnp.int32)
    word = jnp.where(inside, (1 << 30) + ((place - rank) << 16) + local, 0)
    step = 0
    while (1 << step) < top_count:
        moved = pltpu.roll(word, lanes - (1 << step), 1)
        bit = 1 << (16 + step)
        word = jnp.where(
            (moved & bit) != 0, moved, jnp.where((word & bit) != 0, 0, word)
        )
        step += 1
    local = word & 0xFFFF
    low = (local & (LANES - 1)).astype(F32).astype(BF)
    high = jnp.where(word != 0, (local >> 7) + 1, 0).astype(F32).astype(BF)
    both = jnp.concatenate([low, high], axis=0)
    column = iota((tokens, CELL), 1) // slab_most
    own = column == jnp.bitwise_and(iota((tokens, CELL), 0), tokens_cell - 1)
    pool = flag(iota((cells, tokens), 1) // tokens_cell == iota((cells, tokens), 0))
    out = []
    for layer in range(layers):
        pick = flag(
            iota((lanes, CELL), 0)
            == layer * top_count + jnp.bitwise_and(iota((lanes, CELL), 1), slab_most - 1)
        )
        tiled = matmul(both, pick)
        low_t = jnp.where(own, tiled[:tokens], 0.0).astype(BF)
        high_t = jnp.where(own, tiled[tokens:], 0.0).astype(BF)
        low_z = matmul(pool, low_t).astype(jnp.int32)
        high_z = matmul(pool, high_t).astype(jnp.int32)
        token = iota((cells, CELL), 1) // slab_most
        row = (high_z - 1) * tokens_cell + token
        out.append(jnp.where(high_z > 0, row * LANES + low_z, -1))
    return jnp.concatenate(out, axis=0)


def encode_kernel(plan, where_ref, x_ref, encoder_ref, bias_ref, top_ref, z_ref, zidx_ref, slots):
    layers, cells, tokens_cell, width, top_count, slab_most = plan
    depth = encoder_ref.shape[1]
    zidx_ref[...] = slot_index(
        top_ref[...], where_ref[1], width, layers, top_count, slab_most, tokens_cell
    )
    with_bias = jnp.where(where_ref[0] == 0, 1.0, 0.0)
    for layer in range(layers):
        dense = matmul(x_ref[:, layer * depth : (layer + 1) * depth], encoder_ref[layer])
        dense = dense + bias_ref[layer : layer + 1, :] * with_bias
        gather_slots(dense, zidx_ref, slots, layer, cells, tokens_cell, width)
    z_ref[...] = slots[...].astype(BF)


def decode_kernel(plan, pair, parts_ref, zidx_ref, decoder_ref, act_ref, partial_ref):
    layers, cells, tokens_cell, width, top_count, slab_most = plan
    total = jnp.sum(parts_ref[...].astype(F32), axis=0)
    total = total.astype(BF).astype(F32)
    for layer in range(layers):
        scatter_slots(total, zidx_ref, act_ref, layer, cells, tokens_cell, width)
    sums = [None, None]
    for k in range(layers + 1):
        source, slot = (k, 0) if k <= pair else (k - pair - 1, 1)
        term = matmul(act_ref[source], decoder_ref[k])
        sums[slot] = term if sums[slot] is None else sums[slot] + term
    for slot in range(2):
        partial_ref[slot] = sums[slot].astype(BF)


def residue_kernel(
    plan, pair, parts_ref, dec_bias_ref, targets_ref, zidx_ref, decoder_ref, act_ref,
    z_ref, grad_ref, slots, residue
):
    layers, cells, tokens_cell, width, top_count, slab_most = plan
    for slot in range(2):
        rebuilt = jnp.sum(parts_ref[:, slot].astype(F32), axis=0)
        rebuilt = rebuilt + dec_bias_ref[slot : slot + 1, :]
        residue[slot] = (rebuilt - targets_ref[slot].astype(F32)).astype(BF)
    places = [(k, 0) if k <= pair else (k - pair - 1, 1) for k in range(layers + 1)]
    for layer in range(layers):
        dense = None
        for k in range(layers + 1):
            if places[k][0] == layer:
                term = matmul(residue[places[k][1]], decoder_ref[k], NT)
                dense = term if dense is None else dense + term
        if dense is None:
            slots[layer * cells : (layer + 1) * cells, :] = jnp.zeros((cells, CELL), F32)
        else:
            gather_slots(dense, zidx_ref, slots, layer, cells, tokens_cell, width)
    z_ref[...] = slots[...].astype(BF)
    for k in range(layers + 1):
        grad_ref[k] = matmul(act_ref[places[k][0]], residue[places[k][1]], TN)


def encoder_grad_kernel(plan, parts_ref, zidx_ref, x_ref, grad_ref, bias_ref, dense):
    layers, cells, tokens_cell, width, top_count, slab_most = plan
    depth = grad_ref.shape[1]
    tokens = x_ref.shape[0]
    total = jnp.sum(parts_ref[...].astype(F32), axis=0)
    total = total.astype(BF).astype(F32)
    for layer in range(layers):
        scatter_slots(total, zidx_ref, dense, layer, cells, tokens_cell, width)
        grad_ref[layer] = matmul(
            x_ref[:, layer * depth : (layer + 1) * depth], dense[layer], TN
        )
        ones = jnp.ones((8, tokens), BF)
        bias_ref[layer : layer + 1, :] = matmul(ones, dense[layer])[:1]


def call(kernel, out_shape, scratch, *args, smem=0):
    vmem = pl.BlockSpec(memory_space=pltpu.VMEM)
    return pl.pallas_call(
        kernel,
        out_shape=out_shape,
        in_specs=[pl.BlockSpec(memory_space=pltpu.SMEM)] * smem + [vmem] * (len(args) - smem),
        out_specs=jax.tree.map(lambda _: vmem, out_shape),
        scratch_shapes=scratch,
        compiler_params=pltpu.CompilerParams(vmem_limit_bytes=40 * 1024 * 1024),
    )(*args)


def share(value, axis):
    count = lax.axis_size(axis)
    copies = jnp.broadcast_to(value[None], (count,) + value.shape)
    return lax.all_to_all(copies, axis, 0, 0, tiled=True)


def by_pair(pairs, build, *args):
    branches = [functools.partial(build, pair) for pair in range(pairs)]
    if pairs == 1:
        return branches[0](*args)
    return lax.switch(lax.axis_index("layer") // FEAT_SPLIT, branches, *args)


def body(inputs, encoder, enc_bias, decoder, dec_bias, targets, top_index):
    tokens, layers, top_count = top_index.shape
    width = encoder.shape[2]
    feat = decoder.shape[3]
    slab_most = 2 * top_count // lax.axis_size("lat")
    tokens_cell = CELL // slab_most
    cells = tokens // tokens_cell
    rows = layers * cells
    pairs = lax.axis_size("layer") // FEAT_SPLIT
    plan = (layers, cells, tokens_cell, width, top_count, slab_most)
    where = jnp.stack([lax.axis_index("layer"), lax.axis_index("lat")]).astype(jnp.int32)
    x = inputs.reshape(tokens, -1)
    top = top_index.reshape(tokens, -1)
    shape = jax.ShapeDtypeStruct
    z, zidx = call(
        functools.partial(encode_kernel, plan),
        (shape((rows, CELL), BF), shape((rows, CELL), jnp.int32)),
        [pltpu.VMEM((rows, CELL), F32)],
        where, x, encoder, enc_bias, top, smem=1,
    )
    parts = share(z, "layer")

    def decode(pair, *args):
        return call(
            functools.partial(decode_kernel, plan, pair),
            (shape((layers, tokens, width), BF), shape((2, tokens, feat), BF)),
            [],
            *args,
        )

    act, partial = by_pair(pairs, decode, parts, zidx, decoder[0])
    partials = lax.all_gather(partial, "lat")

    def residues(pair, *args):
        return call(
            functools.partial(residue_kernel, plan, pair),
            (shape((rows, CELL), BF), shape((layers + 1, width, feat), F32)),
            [pltpu.VMEM((rows, CELL), F32), pltpu.VMEM((2, tokens, feat), BF)],
            *args,
        )

    z, decoder_grad = by_pair(
        pairs, residues, partials, dec_bias[0], jnp.swapaxes(targets[0], 0, 1), zidx, decoder[0], act
    )
    parts = share(z, "layer")
    encoder_grad, bias_grad = call(
        functools.partial(encoder_grad_kernel, plan),
        (shape(encoder.shape, F32), shape(enc_bias.shape, F32)),
        [pltpu.VMEM((layers, tokens, width), BF)],
        parts, zidx, x,
    )
    return decoder_grad[None], encoder_grad, bias_grad


def solution(mesh):
    return jax.shard_map(
        body,
        mesh=mesh,
        in_specs=(
            P(None, None, "layer"),
            P(None, "layer", "lat"),
            P(None, "lat"),
            P("layer", None, "lat", None),
            P("layer", None, None),
            P("layer", None, None, None),
            P(),
        ),
        out_specs=(P("layer", None, "lat", None), P(None, "layer", "lat"), P(None, "lat")),
        check_vma=False,
    )
```

```python
import functools

import jax
import jax.numpy as jnp
from jax import lax
from jax.experimental import pallas as pl
from jax.experimental.pallas import tpu as pltpu
from jax.sharding import PartitionSpec as P

FEAT_SPLIT = 8
LANES = 128
CELL = 256
PARTS = 4

BF = jnp.bfloat16
F32 = jnp.float32
NT = (((1,), (1,)), ((), ()))
TN = (((0,), (0,)), ((), ()))


def matmul(left, right, dims=(((1,), (0,)), ((), ()))):
    return lax.dot_general(left, right, dims, preferred_element_type=F32)


def flag(condition):
    return jnp.where(condition, 1.0, 0.0).astype(BF)


def iota(shape, dimension):
    return lax.broadcasted_iota(jnp.int32, shape, dimension)


def pick_lanes(table, lanes):
    return jnp.take_along_axis(table, lanes, axis=1, mode="promise_in_bounds")


def choose(options, code):
    bit = 1
    while len(options) > 1:
        odd = (code & bit) != 0
        options = [
            jnp.where(odd, options[i + 1], options[i]) if i + 1 < len(options) else options[i]
            for i in range(0, len(options), 2)
        ]
        bit *= 2
    return options[0]


def stride(width):
    return 1 << (width // LANES - 1).bit_length()


def gather_slots(dense, index):
    lane = jnp.bitwise_and(index, LANES - 1)
    picked = [
        pick_lanes(dense[:, b * LANES : (b + 1) * LANES], lane)
        for b in range(dense.shape[1] // LANES)
    ]
    return choose(picked, lax.shift_right_logical(index, 7))


def join_layers(picked, index, width):
    total = choose(picked, lax.shift_right_logical(index, 7) // stride(width))
    return jnp.where(index < 0, 0.0, total)


def fold_slots(values, used):
    folds = LANES // used
    rows = values.shape[0] // folds
    total = values[:rows]
    for f in range(1, folds):
        total = total + pltpu.roll(values[f * rows : (f + 1) * rows], f * used, 1)
    return total


def unfold_slots(values, used):
    folds = LANES // used
    parts = [values] + [pltpu.roll(values, LANES - f * used, 1) for f in range(1, folds)]
    return jnp.concatenate(parts, axis=0)


def sum_parts(parts_ref, used):
    total = jnp.sum(parts_ref[...].astype(F32), axis=0)
    total = unfold_slots(total.astype(BF).astype(F32), used)
    return jnp.where(iota(total.shape, 1) < used, total, 0.0)


def place_slots(values, lane):
    blocks = lane.shape[1] // LANES
    return jnp.concatenate(
        [pick_lanes(values, lane[:, b * LANES : (b + 1) * LANES]).astype(BF) for b in range(blocks)],
        axis=1,
    )


def slot_index(top, slab, width, layers, top_count, slab_most):
    rows, tokens = top.shape
    place = jnp.bitwise_and(iota(top.shape, 0), top_count - 1)
    local = top - slab * width
    inside = (local >= 0) & (local < width)
    after = iota((rows, rows), 0)
    before = iota((rows, rows), 1)
    earlier = flag((before // top_count == after // top_count) & (before < after))
    rank = matmul(earlier, flag(inside)).astype(jnp.int32)
    local = local + (iota(top.shape, 0) // top_count) * (stride(width) * LANES)
    word = jnp.where(inside, (1 << 30) + ((place - rank) << 16) + local, 0)
    step = 0
    while (1 << step) < top_count:
        moved = pltpu.roll(word, rows - (1 << step), 0)
        bit = 1 << (16 + step)
        word = jnp.where((moved & bit) != 0, moved, jnp.where((word & bit) != 0, 0, word))
        step += 1
    index = jnp.where(word != 0, word & 0xFFFF, -1)
    kept = [index[layer * top_count : layer * top_count + slab_most] for layer in range(layers)]
    spare = LANES - layers * slab_most
    if spare:
        kept.append(jnp.full((spare, tokens), -1, jnp.int32))
    return jnp.transpose(jnp.concatenate(kept, axis=0), (1, 0))


def encode_kernel(
    plan, x_hbm, encoder_hbm, bias_hbm, top_hbm, z_ref, index_ref,
    x_ref, encoder_ref, bias_ref, top_ref, x_layer, sems
):
    layers, width, top_count, slab_most = plan
    copies = [
        pltpu.make_async_copy(source, target, sems.at[i])
        for i, (source, target) in enumerate(
            [(top_hbm, top_ref), (x_hbm, x_ref), (bias_hbm, bias_ref), (encoder_hbm, encoder_ref)]
        )
    ]
    for copy in copies:
        copy.start()
    for copy in copies[:2]:
        copy.wait()
    for layer in range(layers):
        x_layer[layer] = x_ref[:, layer, :]
    index = slot_index(top_ref[...], lax.axis_index("lat"), width, layers, top_count, slab_most)
    index_ref[...] = index
    for copy in copies[2:]:
        copy.wait()
    with_bias = jnp.where(lax.axis_index("layer") == 0, 1.0, 0.0)
    picked = []
    for layer in range(layers):
        dense = matmul(x_layer[layer], encoder_ref[layer])
        dense = dense + bias_ref[layer : layer + 1, :] * with_bias
        picked.append(gather_slots(dense, index))
    z_ref[...] = fold_slots(join_layers(picked, index, width), layers * slab_most).astype(BF)


def inverse_kernel(plan, index_ref, inverse_ref):
    layers, width, top_count, slab_most = plan
    index = index_ref[...]
    tokens = index.shape[0]
    tokens_cell = CELL // slab_most
    cells = tokens // tokens_cell
    blocks = width // LANES
    rows = blocks * tokens_cell
    low = jnp.bitwise_and(index, LANES - 1).astype(F32).astype(BF)
    high = (lax.shift_right_arithmetic(index, 7) + 1).astype(F32).astype(BF)
    both = jnp.concatenate([low, high], axis=0)
    own = iota((tokens, CELL), 1) // slab_most == jnp.bitwise_and(
        iota((tokens, CELL), 0), tokens_cell - 1
    )
    pool = flag(iota((cells, tokens), 1) // tokens_cell == iota((cells, tokens), 0))
    token = iota((cells, CELL), 1) // slab_most
    slot = jnp.bitwise_and(iota((rows, CELL), 1), slab_most - 1)
    for layer in range(layers):
        pick = flag(
            iota((LANES, CELL), 0)
            == layer * slab_most + jnp.bitwise_and(iota((LANES, CELL), 1), slab_most - 1)
        )
        tiled = matmul(both, pick)
        low_c = matmul(pool, jnp.where(own, tiled[:tokens], 0.0).astype(BF)).astype(jnp.int32)
        high_c = matmul(pool, jnp.where(own, tiled[tokens:], 0.0).astype(BF)).astype(jnp.int32)
        row_c = jnp.where(high_c > 0, (high_c - 1 - layer * stride(width)) * tokens_cell + token, -1)
        lane_id = (slot + (layer * slab_most - (LANES - 1))).astype(F32)
        for cell in range(cells):
            row_hit = iota((rows, CELL), 0) == row_c[cell : cell + 1]
            lane_hot = flag(iota((LANES, CELL), 0) == low_c[cell : cell + 1])
            placed = jnp.where(row_hit, lane_id, 0.0).astype(BF)
            view = matmul(placed, lane_hot, NT).astype(jnp.int32) + (LANES - 1)
            for b in range(blocks):
                inverse_ref[
                    layer,
                    cell * tokens_cell : (cell + 1) * tokens_cell,
                    b * LANES : (b + 1) * LANES,
                ] = view[b * tokens_cell : (b + 1) * tokens_cell]


def decode_kernel(
    plan, pair, parts_ref, inverse_ref, decoder_ref, index_ref, act_ref, partial_ref, index_out
):
    index_out[...] = index_ref[...]
    layers, width, top_count, slab_most = plan
    total = sum_parts(parts_ref, layers * slab_most)
    for layer in range(layers):
        act_ref[layer] = place_slots(total, inverse_ref[layer])
    sums = [None, None]
    for k in range(layers + 1):
        source, slot = (k, 0) if k <= pair else (k - pair - 1, 1)
        term = matmul(act_ref[source], decoder_ref[k])
        sums[slot] = term if sums[slot] is None else sums[slot] + term
    for slot in range(2):
        partial_ref[slot] = sums[slot].astype(BF)


def residue_kernel(
    plan, pair, parts_ref, dec_bias_ref, targets_ref, index_ref, decoder_ref, z_ref, residue
):
    layers, width, top_count, slab_most = plan
    for slot in range(2):
        rebuilt = jnp.sum(parts_ref[:, slot].astype(F32), axis=0)
        rebuilt = rebuilt + dec_bias_ref[slot : slot + 1, :]
        residue[slot] = (rebuilt - targets_ref[slot].astype(F32)).astype(BF)
    places = [(k, 0) if k <= pair else (k - pair - 1, 1) for k in range(layers + 1)]
    index = index_ref[...]
    picked = []
    for layer in range(layers):
        dense = None
        for k in range(layers + 1):
            if places[k][0] == layer:
                term = matmul(residue[places[k][1]], decoder_ref[k], NT)
                dense = term if dense is None else dense + term
        picked.append(jnp.zeros(index.shape, F32) if dense is None else gather_slots(dense, index))
    z_ref[...] = fold_slots(join_layers(picked, index, width), layers * slab_most).astype(BF)


def decoder_grad_kernel(plan, pair, act_ref, residue_ref, x_ref, grad_hbm, xt_ref, grad, sems):
    layers = plan[0]
    copies = []
    for k in range(layers + 1):
        source, slot = (k, 0) if k <= pair else (k - pair - 1, 1)
        grad[k] = matmul(act_ref[source], residue_ref[slot], TN)
        copy = pltpu.make_async_copy(grad.at[k], grad_hbm.at[k], sems.at[k])
        copy.start()
        copies.append(copy)
    for layer in range(layers):
        xt_ref[layer] = jnp.transpose(x_ref[:, layer, :], (1, 0))
    for copy in copies:
        copy.wait()


def encoder_grad_kernel(
    plan, parts_ref, inverse_ref, xt_ref, grad_hbm, bias_hbm, values, grad, bias, sems, bias_sem
):
    layers, width, top_count, slab_most = plan
    tokens = xt_ref.shape[2]
    part = width // PARTS
    values[...] = sum_parts(parts_ref, layers * slab_most)
    ones = jnp.ones((8, tokens), BF)
    copies = []
    for layer in range(layers):
        for i in range(PARTS):
            at = (layer, slice(None), pl.ds(i * part, part))
            dense = place_slots(values[...], inverse_ref[at])
            grad[at] = matmul(xt_ref[layer], dense)
            copies.append(
                pltpu.make_async_copy(grad.at[at], grad_hbm.at[at], sems.at[layer * PARTS + i])
            )
            copies[-1].start()
            bias[layer : layer + 1, i * part : (i + 1) * part] = matmul(ones, dense)[:1]
    copies.append(pltpu.make_async_copy(bias, bias_hbm, bias_sem))
    copies[-1].start()
    for copy in copies:
        copy.wait()


VMEM = pl.BlockSpec(memory_space=pltpu.VMEM)
HBM = pl.BlockSpec(memory_space=pltpu.HBM)
MIB = 1024 * 1024


def call(kernel, ins, outs, scratch, *args, cost=None, room=24):
    args = [
        pltpu.with_memory_space_constraint(arg, pltpu.HBM) if spec is HBM else arg
        for spec, arg in zip(ins, args, strict=True)
    ]
    return pl.pallas_call(
        kernel,
        out_shape=tuple(
            (pltpu.HBM if spec is HBM else pltpu.VMEM)(shape, dtype) for shape, dtype, spec in outs
        ),
        in_specs=ins,
        out_specs=tuple(spec for _, _, spec in outs),
        scratch_shapes=scratch,
        cost_estimate=cost,
        compiler_params=pltpu.CompilerParams(vmem_limit_bytes=room * MIB),
    )(*args)


def share(value, axis):
    copies = jnp.broadcast_to(value[None], (lax.axis_size(axis),) + value.shape)
    return lax.all_to_all(copies, axis, 0, 0, tiled=True)


def by_pair(pairs, build, *args):
    branches = [functools.partial(build, pair) for pair in range(pairs)]
    if pairs == 1:
        return branches[0](*args)
    return lax.switch(lax.axis_index("layer") // FEAT_SPLIT, branches, *args)


def body(inputs, encoder, enc_bias, decoder, dec_bias, targets, top_index):
    tokens, layers, top_count = top_index.shape
    depth, width = encoder.shape[1:]
    feat = decoder.shape[3]
    slab_most = 2 * top_count // lax.axis_size("lat")
    packed = tokens * layers * slab_most // LANES
    pairs = lax.axis_size("layer") // FEAT_SPLIT
    plan = (layers, width, top_count, slab_most)
    top = jnp.transpose(top_index, (1, 2, 0)).reshape(layers * top_count, tokens)
    dma = pltpu.SemaphoreType.DMA
    i32 = jnp.int32
    z, index = call(
        functools.partial(encode_kernel, plan),
        [HBM] * 4,
        [((packed, LANES), BF, VMEM), ((tokens, LANES), i32, VMEM)],
        [
            pltpu.VMEM(inputs.shape, BF),
            pltpu.VMEM(encoder.shape, BF),
            pltpu.VMEM(enc_bias.shape, F32),
            pltpu.VMEM(top.shape, i32),
            pltpu.VMEM((layers, tokens, depth), BF),
            dma((4,)),
        ],
        inputs, encoder, enc_bias, top,
    )
    parts = share(z, "layer")
    (inverse,) = call(
        functools.partial(inverse_kernel, plan),
        [VMEM],
        [((layers, tokens, width), i32, VMEM)],
        [],
        index,
        cost=pl.CostEstimate(flops=10**8, bytes_accessed=10**6, transcendentals=0),
    )

    def decode(pair, *args):
        return call(
            functools.partial(decode_kernel, plan, pair),
            [VMEM] * 4,
            [
                ((layers, tokens, width), BF, VMEM),
                ((2, tokens, feat), BF, VMEM),
                ((tokens, LANES), i32, VMEM),
            ],
            [],
            *args,
        )

    act, partial, index = by_pair(pairs, decode, parts, inverse, decoder[0], index)
    partials = lax.all_gather(partial, "lat")

    def residues(pair, *args):
        return call(
            functools.partial(residue_kernel, plan, pair),
            [VMEM] * 5,
            [((packed, LANES), BF, VMEM), ((2, tokens, feat), BF, VMEM)],
            [],
            *args,
        )

    z, residue = by_pair(
        pairs, residues, partials, dec_bias[0], jnp.swapaxes(targets[0], 0, 1), index, decoder[0]
    )
    parts = share(z, "layer")

    def decoder_grads(pair, *args):
        return call(
            functools.partial(decoder_grad_kernel, plan, pair),
            [VMEM] * 3,
            [((layers + 1, width, feat), F32, HBM), ((layers, depth, tokens), BF, VMEM)],
            [pltpu.VMEM((layers + 1, width, feat), F32), dma((layers + 1,))],
            *args,
            cost=pl.CostEstimate(
                flops=2 * (layers + 1) * tokens * width * feat,
                bytes_accessed=4 * (layers + 1) * width * feat,
                transcendentals=0,
            ),
        )

    decoder_grad, xt = by_pair(pairs, decoder_grads, act, residue, inputs)
    encoder_grad, bias_grad = call(
        functools.partial(encoder_grad_kernel, plan),
        [VMEM] * 3,
        [(encoder.shape, F32, HBM), (enc_bias.shape, F32, HBM)],
        [
            pltpu.VMEM((tokens, LANES), F32),
            pltpu.VMEM(encoder.shape, F32),
            pltpu.VMEM(enc_bias.shape, F32),
            dma((PARTS * layers,)),
            dma,
        ],
        parts, inverse, xt,
    )
    return decoder_grad[None], encoder_grad, bias_grad


def solution(mesh):
    return jax.shard_map(
        body,
        mesh=mesh,
        in_specs=(
            P(None, None, "layer"),
            P(None, "layer", "lat"),
            P(None, "lat"),
            P("layer", None, "lat", None),
            P("layer", None, None),
            P("layer", None, None, None),
            P(),
        ),
        out_specs=(P("layer", None, "lat", None), P(None, "layer", "lat"), P(None, "lat")),
        check_vma=False,
    )
```

```python
import functools

import jax
import jax.numpy as jnp
from jax import lax
from jax.experimental import pallas as pl
from jax.experimental.pallas import tpu as pltpu
from jax.sharding import PartitionSpec as P

FEAT_SPLIT = 8
LANES = 128
PARTS = 4
CHUNK = 32
NUMBER_BITS = 7
WORD_BLOCKS = 31 // NUMBER_BITS

BF = jnp.bfloat16
F32 = jnp.float32
NT = (((1,), (1,)), ((), ()))
TN = (((0,), (0,)), ((), ()))


def matmul(left, right, dims=(((1,), (0,)), ((), ()))):
    return lax.dot_general(left, right, dims, preferred_element_type=F32)


def flag(condition):
    return jnp.where(condition, 1.0, 0.0).astype(BF)


def iota(shape, dimension):
    return lax.broadcasted_iota(jnp.int32, shape, dimension)


def pick_lanes(table, lanes):
    return jnp.take_along_axis(table, lanes, axis=1, mode="promise_in_bounds")


def choose(options, code):
    bit = 1
    while len(options) > 1:
        odd = (code & bit) != 0
        options = [
            jnp.where(odd, options[i + 1], options[i]) if i + 1 < len(options) else options[i]
            for i in range(0, len(options), 2)
        ]
        bit *= 2
    return options[0]


def stride(width):
    return 1 << (width // LANES - 1).bit_length()


def gather_slots(dense, index):
    lane = jnp.bitwise_and(index, LANES - 1)
    picked = [
        pick_lanes(dense[:, b * LANES : (b + 1) * LANES], lane)
        for b in range(dense.shape[1] // LANES)
    ]
    return choose(picked, lax.shift_right_logical(index, 7))


def join_layers(picked, index, width):
    total = choose(picked, lax.shift_right_logical(index, 7) // stride(width))
    return jnp.where(index < 0, 0.0, total)


def fold_slots(values, used):
    folds = LANES // used
    rows = values.shape[0] // folds
    total = values[:rows]
    for f in range(1, folds):
        total = total + pltpu.roll(values[f * rows : (f + 1) * rows], f * used, 1)
    return total


def sum_parts(parts_ref, used):
    total = jnp.sum(parts_ref[...].astype(F32), axis=0).astype(BF).astype(F32)
    folds = LANES // used
    total = jnp.concatenate(
        [pltpu.roll(total, (1 - f * used) % LANES, 1) for f in range(folds)], axis=0
    )
    lane = iota(total.shape, 1)
    return jnp.where((lane > 0) & (lane <= used), total, 0.0)


def place_slots(values, lane):
    blocks = lane.shape[1] // LANES
    return jnp.concatenate(
        [pick_lanes(values, lane[:, b * LANES : (b + 1) * LANES]).astype(BF) for b in range(blocks)],
        axis=1,
    )


def slot_index(top, slab, width, layers, top_count, slab_most):
    rows, tokens = top.shape
    place = jnp.bitwise_and(iota(top.shape, 0), top_count - 1)
    local = top - slab * width
    inside = (local >= 0) & (local < width)
    after = iota((rows, rows), 0)
    before = iota((rows, rows), 1)
    earlier = flag((before // top_count == after // top_count) & (before < after))
    rank = matmul(earlier, flag(inside)).astype(jnp.int32)
    local = local + (iota(top.shape, 0) // top_count) * (stride(width) * LANES)
    word = jnp.where(inside, (1 << 30) + ((place - rank) << 16) + local, 0)
    step = 0
    while (1 << step) < top_count:
        moved = pltpu.roll(word, rows - (1 << step), 0)
        bit = 1 << (16 + step)
        word = jnp.where((moved & bit) != 0, moved, jnp.where((word & bit) != 0, 0, word))
        step += 1
    index = jnp.where(word != 0, word & 0xFFFF, -1)
    return jnp.concatenate(
        [index[layer * top_count : layer * top_count + slab_most] for layer in range(layers)], axis=0
    )


def by_token(kept):
    spare = jnp.full((LANES - kept.shape[0], kept.shape[1]), -1, jnp.int32)
    return jnp.transpose(jnp.concatenate([kept, spare], axis=0), (1, 0))


def inverse_kernel(plan, kept_ref, inverse_ref, rows_ref):
    layers, width, top_count, slab_most = plan
    tokens = kept_ref.shape[1]
    blocks = width // LANES
    words = -(-blocks // WORD_BLOCKS)
    for layer in range(layers):
        own = kept_ref[layer * slab_most : (layer + 1) * slab_most, :]
        block = lax.shift_right_arithmetic(own, 7) - layer * stride(width)
        number = iota(own.shape, 0) + (1 + layer * slab_most)
        value = lax.shift_left(number, NUMBER_BITS * (block % WORD_BLOCKS))
        rows_ref[layer, 0] = jnp.bitwise_and(own, LANES - 1)
        for w in range(words):
            rows_ref[layer, 1 + w] = jnp.where((own >= 0) & (block // WORD_BLOCKS == w), value, 0)
        pieces = [[] for w in range(words)]
        for first in range(0, LANES, CHUNK):
            lane = iota((CHUNK, tokens), 0) + first
            totals = [jnp.zeros((CHUNK, tokens), jnp.int32) for w in range(words)]
            for s in range(slab_most):
                match = lane == rows_ref[layer, 0, s : s + 1, :]
                for w in range(words):
                    totals[w] = totals[w] + jnp.where(match, rows_ref[layer, 1 + w, s : s + 1, :], 0)
            for w in range(words):
                pieces[w].append(totals[w])
        for w in range(words):
            word = jnp.transpose(jnp.concatenate(pieces[w], axis=0), (1, 0))
            for b in range(w * WORD_BLOCKS, min((w + 1) * WORD_BLOCKS, blocks)):
                numbers = lax.shift_right_logical(word, NUMBER_BITS * (b % WORD_BLOCKS))
                inverse_ref[layer, :, b * LANES : (b + 1) * LANES] = jnp.bitwise_and(
                    numbers, LANES - 1
                )


def encode_kernel(
    plan, x_hbm, encoder_hbm, bias_hbm, top_hbm, z_ref, index_ref, kept_ref,
    x_ref, encoder_ref, bias_ref, top_ref, x_layer, sems
):
    layers, width, top_count, slab_most = plan
    copies = [
        pltpu.make_async_copy(source, target, sems.at[i])
        for i, (source, target) in enumerate(
            [(top_hbm, top_ref), (x_hbm, x_ref), (bias_hbm, bias_ref), (encoder_hbm, encoder_ref)]
        )
    ]
    for copy in copies:
        copy.start()
    for copy in copies[:2]:
        copy.wait()
    for layer in range(layers):
        x_layer[layer] = x_ref[:, layer, :]
    kept = slot_index(top_ref[...], lax.axis_index("lat"), width, layers, top_count, slab_most)
    kept_ref[...] = kept
    index = by_token(kept)
    index_ref[...] = index
    for copy in copies[2:]:
        copy.wait()
    with_bias = jnp.where(lax.axis_index("layer") == 0, 1.0, 0.0)
    picked = []
    for layer in range(layers):
        dense = matmul(x_layer[layer], encoder_ref[layer])
        dense = dense + bias_ref[layer : layer + 1, :] * with_bias
        picked.append(gather_slots(dense, index))
    z_ref[...] = fold_slots(join_layers(picked, index, width), layers * slab_most).astype(BF)


def block_places(layers, pair):
    return [(k, 0) if k <= pair else (k - pair - 1, 1) for k in range(layers + 1)]


def decode_kernel(
    plan, pair, parts_ref, inverse_ref, decoder_ref, index_ref, act_ref, partial_ref, index_out
):
    layers, width, top_count, slab_most = plan
    index_out[...] = index_ref[...]
    total = sum_parts(parts_ref, layers * slab_most)
    for layer in range(layers):
        act_ref[layer] = place_slots(total, inverse_ref[layer])
    sums = [None, None]
    for k, (source, slot) in enumerate(block_places(layers, pair)):
        term = matmul(act_ref[source], decoder_ref[k])
        sums[slot] = term if sums[slot] is None else sums[slot] + term
    for slot in range(2):
        partial_ref[slot] = sums[slot].astype(BF)


def turn_kernel(act_ref, x_ref, targets_ref, decoder_ref, act_t, x_t, targets_out, decoder_t):
    for layer in range(act_ref.shape[0]):
        act_t[layer] = jnp.transpose(act_ref[layer], (1, 0))
        x_t[layer] = jnp.transpose(x_ref[:, layer, :], (1, 0))
    for slot in range(2):
        targets_out[slot] = targets_ref[:, slot, :]
    for k in range(decoder_ref.shape[0]):
        decoder_t[k] = jnp.transpose(decoder_ref[k], (1, 0))


def residue_kernel(
    plan, pair, mine_ref, theirs_ref, dec_bias_ref, targets_ref, index_ref, decoder_t,
    z_ref, residue
):
    layers, width, top_count, slab_most = plan
    for slot in range(2):
        rebuilt = mine_ref[slot].astype(F32) + theirs_ref[slot].astype(F32)
        rebuilt = rebuilt + dec_bias_ref[slot : slot + 1, :]
        residue[slot] = (rebuilt - targets_ref[slot].astype(F32)).astype(BF)
    places = block_places(layers, pair)
    index = index_ref[...]
    picked = []
    for layer in range(layers):
        dense = None
        for k, (source, slot) in enumerate(places):
            if source == layer:
                term = matmul(residue[slot], decoder_t[k])
                dense = term if dense is None else dense + term
        picked.append(jnp.zeros(index.shape, F32) if dense is None else gather_slots(dense, index))
    z_ref[...] = fold_slots(join_layers(picked, index, width), layers * slab_most).astype(BF)


def grads_kernel(
    plan, pair, parts_ref, inverse_ref, x_t, act_t, residue_ref,
    decoder_hbm, encoder_hbm, bias_hbm, values, decoder_grad, encoder_grad, bias, sems
):
    layers, width, top_count, slab_most = plan
    tokens = x_t.shape[2]
    part = width // PARTS
    copies = []

    def send(source, target):
        copies.append(pltpu.make_async_copy(source, target, sems.at[len(copies)]))
        copies[-1].start()

    for k, (source, slot) in enumerate(block_places(layers, pair)):
        decoder_grad[k] = matmul(act_t[source], residue_ref[slot])
        send(decoder_grad.at[k], decoder_hbm.at[k])
    values[...] = sum_parts(parts_ref, layers * slab_most)
    ones = jnp.ones((8, tokens), BF)
    for layer in range(layers):
        for i in range(PARTS):
            at = (layer, slice(None), pl.ds(i * part, part))
            dense = place_slots(values[...], inverse_ref[at])
            encoder_grad[at] = matmul(x_t[layer], dense)
            send(encoder_grad.at[at], encoder_hbm.at[at])
            bias[layer : layer + 1, i * part : (i + 1) * part] = matmul(ones, dense)[:1]
    send(bias, bias_hbm)
    for copy in copies:
        copy.wait()


VMEM = pl.BlockSpec(memory_space=pltpu.VMEM)
HBM = pl.BlockSpec(memory_space=pltpu.HBM)
MIB = 1024 * 1024


def call(kernel, ins, outs, scratch, *args, cost=None, room=24):
    args = [
        pltpu.with_memory_space_constraint(arg, pltpu.HBM) if spec is HBM else arg
        for spec, arg in zip(ins, args, strict=True)
    ]
    return pl.pallas_call(
        kernel,
        out_shape=tuple(
            (pltpu.HBM if spec is HBM else pltpu.VMEM)(shape, dtype) for shape, dtype, spec in outs
        ),
        in_specs=ins,
        out_specs=tuple(spec for _, _, spec in outs),
        scratch_shapes=scratch,
        cost_estimate=cost,
        compiler_params=pltpu.CompilerParams(vmem_limit_bytes=room * MIB),
    )(*args)


def share(value, axis):
    copies = jnp.broadcast_to(value[None], (lax.axis_size(axis),) + value.shape)
    return lax.all_to_all(copies, axis, 0, 0, tiled=True)


def by_pair(pairs, build, *args):
    branches = [functools.partial(build, pair) for pair in range(pairs)]
    if pairs == 1:
        return branches[0](*args)
    return lax.switch(lax.axis_index("layer") // FEAT_SPLIT, branches, *args)


def across(value, axis, step):
    pairs = [(i, i ^ step) for i in range(lax.axis_size(axis))]
    return lax.ppermute(value, axis, pairs)


def body(inputs, encoder, enc_bias, decoder, dec_bias, targets, top_index):
    tokens, layers, top_count = top_index.shape
    depth, width = encoder.shape[1:]
    feat = decoder.shape[3]
    slabs = lax.axis_size("lat")
    slab_most = 2 * top_count // slabs
    packed = tokens * layers * slab_most // LANES
    pairs = lax.axis_size("layer") // FEAT_SPLIT
    plan = (layers, width, top_count, slab_most)
    top = jnp.transpose(top_index, (1, 2, 0)).reshape(layers * top_count, tokens)
    dma = pltpu.SemaphoreType.DMA
    i32 = jnp.int32
    z, index, kept = call(
        functools.partial(encode_kernel, plan),
        [HBM] * 4,
        [
            ((packed, LANES), BF, VMEM),
            ((tokens, LANES), i32, VMEM),
            ((layers * slab_most, tokens), i32, VMEM),
        ],
        [
            pltpu.VMEM(inputs.shape, BF),
            pltpu.VMEM(encoder.shape, BF),
            pltpu.VMEM(enc_bias.shape, F32),
            pltpu.VMEM(top.shape, i32),
            pltpu.VMEM((layers, tokens, depth), BF),
            dma((4,)),
        ],
        inputs, encoder, enc_bias, top,
    )
    parts = share(z, "layer")
    (inverse,) = call(
        functools.partial(inverse_kernel, plan),
        [VMEM],
        [((layers, tokens, width), i32, VMEM)],
        [pltpu.VMEM((layers, 1 - (-width // (LANES * WORD_BLOCKS)), slab_most, tokens), i32)],
        kept,
        cost=pl.CostEstimate(flops=10**8, bytes_accessed=10**6, transcendentals=0),
    )

    def decode(pair, *args):
        return call(
            functools.partial(decode_kernel, plan, pair),
            [VMEM] * 4,
            [
                ((layers, tokens, width), BF, VMEM),
                ((2, tokens, feat), BF, VMEM),
                ((tokens, LANES), i32, VMEM),
            ],
            [],
            *args,
        )

    act, partial, index = by_pair(pairs, decode, parts, inverse, decoder[0], index)
    step = 1
    while 2 * step < slabs:
        partial = (partial.astype(F32) + across(partial, "lat", step).astype(F32)).astype(BF)
        step *= 2
    partial, act = lax.optimization_barrier((partial, act))
    theirs = across(partial, "lat", step)
    act_t, x_t, targets_by_slot, decoder_t = call(
        turn_kernel,
        [VMEM] * 4,
        [
            ((layers, width, tokens), BF, VMEM),
            ((layers, depth, tokens), BF, VMEM),
            ((2, tokens, feat), BF, VMEM),
            ((layers + 1, feat, width), BF, VMEM),
        ],
        [],
        act, inputs, targets[0], decoder[0],
        cost=pl.CostEstimate(flops=10**8, bytes_accessed=10**7, transcendentals=0),
    )

    def residues(pair, *args):
        return call(
            functools.partial(residue_kernel, plan, pair),
            [VMEM] * 6,
            [((packed, LANES), BF, VMEM), ((2, tokens, feat), BF, VMEM)],
            [],
            *args,
        )

    z, residue = by_pair(
        pairs, residues, partial, theirs, dec_bias[0], targets_by_slot, index, decoder_t
    )
    parts = share(z, "layer")

    def grads(pair, *args):
        return call(
            functools.partial(grads_kernel, plan, pair),
            [VMEM] * 5,
            [
                ((layers + 1, width, feat), F32, HBM),
                (encoder.shape, F32, HBM),
                (enc_bias.shape, F32, HBM),
            ],
            [
                pltpu.VMEM((tokens, LANES), F32),
                pltpu.VMEM((layers + 1, width, feat), F32),
                pltpu.VMEM(encoder.shape, F32),
                pltpu.VMEM(enc_bias.shape, F32),
                dma((PARTS * layers + layers + 2,)),
            ],
            *args,
        )

    decoder_grad, encoder_grad, bias_grad = by_pair(
        pairs, grads, parts, inverse, x_t, act_t, residue
    )
    return decoder_grad[None], encoder_grad, bias_grad


def solution(mesh):
    return jax.shard_map(
        body,
        mesh=mesh,
        in_specs=(
            P(None, None, "layer"),
            P(None, "layer", "lat"),
            P(None, "lat"),
            P("layer", None, "lat", None),
            P("layer", None, None),
            P("layer", None, None, None),
            P(),
        ),
        out_specs=(P("layer", None, "lat", None), P(None, "layer", "lat"), P(None, "lat")),
        check_vma=False,
    )
```

```python
import functools

import jax
import jax.numpy as jnp
from jax import lax
from jax.experimental import pallas as pl
from jax.experimental.pallas import tpu as pltpu
from jax.sharding import PartitionSpec as P

FEAT_SPLIT = 8
LANES = 128
PARTS = 4
CHUNK = 32
NUMBER_BITS = 7
WORD_BLOCKS = 31 // NUMBER_BITS

BF = jnp.bfloat16
F32 = jnp.float32
NT = (((1,), (1,)), ((), ()))
TN = (((0,), (0,)), ((), ()))


def matmul(left, right, dims=(((1,), (0,)), ((), ()))):
    return lax.dot_general(left, right, dims, preferred_element_type=F32)


def flag(condition):
    return jnp.where(condition, 1.0, 0.0).astype(BF)


def iota(shape, dimension):
    return lax.broadcasted_iota(jnp.int32, shape, dimension)


def pick_lanes(table, lanes):
    return lax.gather(
        table,
        lanes[..., None],
        lax.GatherDimensionNumbers(
            offset_dims=(),
            collapsed_slice_dims=(1,),
            start_index_map=(1,),
            operand_batching_dims=(0,),
            start_indices_batching_dims=(0,),
        ),
        slice_sizes=(1, 1),
        mode=lax.GatherScatterMode.PROMISE_IN_BOUNDS,
    )


def choose(options, index, bit):
    while len(options) > 1:
        odd = jnp.bitwise_and(index, jnp.int16(bit)) != 0
        options = [
            jnp.where(odd, options[i + 1], options[i]) if i + 1 < len(options) else options[i]
            for i in range(0, len(options), 2)
        ]
        bit *= 2
    return options[0]


def stride(width):
    return 1 << (width // LANES - 1).bit_length()


def gather_slots(dense, index):
    lane = jnp.bitwise_and(index, jnp.int16(LANES - 1))
    picked = [
        pick_lanes(dense[:, b * LANES : (b + 1) * LANES].astype(BF), lane)
        for b in range(dense.shape[1] // LANES)
    ]
    return choose(picked, index, LANES)


def join_layers(picked, index, width):
    total = choose(picked, index, LANES * stride(width))
    return jnp.where(index < 0, jnp.zeros_like(total), total).astype(F32)


def fold_slots(values, used):
    folds = LANES // used
    rows = values.shape[0] // folds
    total = values[:rows]
    for f in range(1, folds):
        total = total + pltpu.roll(values[f * rows : (f + 1) * rows], f * used, 1)
    return total


def sum_parts(parts_ref, used):
    total = jnp.sum(parts_ref[...].astype(F32), axis=0)
    folds = LANES // used
    total = jnp.concatenate(
        [pltpu.roll(total, (1 - f * used) % LANES, 1) for f in range(folds)], axis=0
    )
    lane = iota(total.shape, 1)
    return jnp.where((lane > 0) & (lane <= used), total, 0.0).astype(BF)


def place_slots(values, lane):
    blocks = lane.shape[1] // LANES
    return jnp.concatenate(
        [pick_lanes(values, lane[:, b * LANES : (b + 1) * LANES]) for b in range(blocks)],
        axis=1,
    )


def slot_index(top, slab, width, layers, top_count, slab_most):
    rows, tokens = top.shape
    place = jnp.bitwise_and(iota(top.shape, 0), top_count - 1)
    local = top - slab * width
    inside = (local >= 0) & (local < width)
    after = iota((rows, rows), 0)
    before = iota((rows, rows), 1)
    earlier = flag((before // top_count == after // top_count) & (before < after))
    rank = matmul(earlier, flag(inside)).astype(jnp.int32)
    local = local + (iota(top.shape, 0) // top_count) * (stride(width) * LANES)
    word = jnp.where(inside, (1 << 30) + ((place - rank) << 16) + local, 0)
    step = 0
    while (1 << step) < top_count:
        moved = pltpu.roll(word, rows - (1 << step), 0)
        bit = 1 << (16 + step)
        word = jnp.where((moved & bit) != 0, moved, jnp.where((word & bit) != 0, 0, word))
        step += 1
    index = jnp.where(word != 0, word & 0xFFFF, -1)
    return jnp.concatenate(
        [index[layer * top_count : layer * top_count + slab_most] for layer in range(layers)], axis=0
    )


def by_token(kept):
    spare = jnp.full((LANES - kept.shape[0], kept.shape[1]), -1, jnp.int32)
    return jnp.transpose(jnp.concatenate([kept, spare], axis=0), (1, 0))


def inverse_kernel(plan, kept_ref, inverse_ref, rows_ref):
    layers, width, top_count, slab_most = plan
    tokens = kept_ref.shape[1]
    blocks = width // LANES
    words = -(-blocks // WORD_BLOCKS)
    for layer in range(layers):
        own = kept_ref[layer * slab_most : (layer + 1) * slab_most, :]
        block = lax.shift_right_arithmetic(own, 7) - layer * stride(width)
        number = iota(own.shape, 0) + (1 + layer * slab_most)
        value = lax.shift_left(number, NUMBER_BITS * (block % WORD_BLOCKS))
        rows_ref[layer, 0] = jnp.bitwise_and(own, LANES - 1)
        for w in range(words):
            rows_ref[layer, 1 + w] = jnp.where((own >= 0) & (block // WORD_BLOCKS == w), value, 0)
        pieces = [[] for w in range(words)]
        for first in range(0, LANES, CHUNK):
            lane = iota((CHUNK, tokens), 0) + first
            totals = [jnp.zeros((CHUNK, tokens), jnp.int32) for w in range(words)]
            for s in range(slab_most):
                match = lane == rows_ref[layer, 0, s : s + 1, :]
                for w in range(words):
                    totals[w] = totals[w] + jnp.where(match, rows_ref[layer, 1 + w, s : s + 1, :], 0)
            for w in range(words):
                pieces[w].append(totals[w])
        for w in range(words):
            word = jnp.transpose(jnp.concatenate(pieces[w], axis=0), (1, 0))
            for b in range(w * WORD_BLOCKS, min((w + 1) * WORD_BLOCKS, blocks)):
                numbers = lax.shift_right_logical(word, NUMBER_BITS * (b % WORD_BLOCKS))
                inverse_ref[layer, :, b * LANES : (b + 1) * LANES] = jnp.bitwise_and(
                    numbers, LANES - 1
                ).astype(jnp.int16)


def encode_kernel(
    plan, x_hbm, encoder_hbm, bias_hbm, top_hbm, z_ref, index_ref, kept_ref,
    x_ref, encoder_ref, bias_ref, top_ref, x_layer, sems
):
    layers, width, top_count, slab_most = plan
    copies = [
        pltpu.make_async_copy(source, target, sems.at[i])
        for i, (source, target) in enumerate(
            [(top_hbm, top_ref), (x_hbm, x_ref), (bias_hbm, bias_ref), (encoder_hbm, encoder_ref)]
        )
    ]
    for copy in copies:
        copy.start()
    for copy in copies[:2]:
        copy.wait()
    tokens, depth = x_ref.shape[0], x_ref.shape[2]
    x_rows = x_ref[...].reshape(tokens * layers, depth)
    token, row = iota((tokens, tokens * layers), 0), iota((tokens, tokens * layers), 1)
    for layer in range(layers):
        x_layer[layer] = matmul(flag(row == layers * token + layer), x_rows).astype(BF)
    kept = slot_index(top_ref[...], lax.axis_index("lat"), width, layers, top_count, slab_most)
    kept_ref[...] = kept
    index = by_token(kept).astype(jnp.int16)
    index_ref[...] = index
    for copy in copies[2:]:
        copy.wait()
    with_bias = jnp.where(lax.axis_index("layer") == 0, 1.0, 0.0)
    picked = []
    for layer in range(layers):
        dense = matmul(x_layer[layer], encoder_ref[layer])
        dense = dense + bias_ref[layer : layer + 1, :] * with_bias
        picked.append(gather_slots(dense, index))
    z_ref[...] = fold_slots(join_layers(picked, index, width), layers * slab_most).astype(BF)


def block_places(layers, pair):
    return [(k, 0) if k <= pair else (k - pair - 1, 1) for k in range(layers + 1)]


def decode_kernel(
    plan, pair, parts_ref, inverse_ref, decoder_ref, index_ref,
    act_ref, partial_ref, rounded_ref, index_out
):
    layers, width, top_count, slab_most = plan
    index_out[...] = index_ref[...]
    total = sum_parts(parts_ref, layers * slab_most)
    for layer in range(layers):
        act_ref[layer] = place_slots(total, inverse_ref[layer])
    sums = [None, None]
    for k, (source, slot) in enumerate(block_places(layers, pair)):
        term = matmul(act_ref[source], decoder_ref[k])
        sums[slot] = term if sums[slot] is None else sums[slot] + term
    for slot in range(2):
        partial_ref[slot] = sums[slot]
        rounded_ref[slot] = sums[slot].astype(BF)


def turn_kernel(act_ref, x_ref, targets_ref, decoder_ref, act_t, x_t, targets_out, decoder_t):
    for layer in range(act_ref.shape[0]):
        act_t[layer] = jnp.transpose(act_ref[layer], (1, 0))
        x_t[layer] = jnp.transpose(x_ref[:, layer, :], (1, 0))
    for slot in range(2):
        targets_out[slot] = targets_ref[:, slot, :]
    for k in range(decoder_ref.shape[0]):
        decoder_t[k] = jnp.transpose(decoder_ref[k], (1, 0))


def residue_kernel(
    plan, pair, mine_ref, theirs_ref, dec_bias_ref, targets_ref, index_ref, decoder_t,
    z_ref, residue
):
    layers, width, top_count, slab_most = plan
    for slot in range(2):
        rebuilt = mine_ref[slot] + theirs_ref[slot].astype(F32)
        rebuilt = rebuilt + dec_bias_ref[slot : slot + 1, :]
        residue[slot] = (rebuilt - targets_ref[slot].astype(F32)).astype(BF)
    places = block_places(layers, pair)
    index = index_ref[...]
    picked = []
    for layer in range(layers):
        dense = None
        for k, (source, slot) in enumerate(places):
            if source == layer:
                term = matmul(residue[slot], decoder_t[k])
                dense = term if dense is None else dense + term
        picked.append(jnp.zeros(index.shape, BF) if dense is None else gather_slots(dense, index))
    z_ref[...] = fold_slots(join_layers(picked, index, width), layers * slab_most).astype(BF)


def grads_kernel(
    plan, pair, parts_ref, inverse_ref, x_t, act_t, residue_ref,
    decoder_hbm, encoder_hbm, bias_hbm, values, decoder_grad, encoder_grad, bias, sems
):
    layers, width, top_count, slab_most = plan
    tokens = x_t.shape[2]
    part = width // PARTS
    copies = []

    def send(source, target):
        copies.append(pltpu.make_async_copy(source, target, sems.at[len(copies)]))
        copies[-1].start()

    for k, (source, slot) in enumerate(block_places(layers, pair)):
        for i in range(PARTS):
            rows = pl.ds(i * part, part)
            decoder_grad[k, rows] = matmul(act_t[source, rows], residue_ref[slot])
            send(decoder_grad.at[k, rows], decoder_hbm.at[k, rows])
    values[...] = sum_parts(parts_ref, layers * slab_most)
    ones = jnp.ones((8, tokens), BF)
    for layer in range(layers):
        for i in range(PARTS):
            at = (layer, slice(None), pl.ds(i * part, part))
            dense = place_slots(values[...], inverse_ref[at])
            encoder_grad[at] = matmul(x_t[layer], dense)
            send(encoder_grad.at[at], encoder_hbm.at[at])
            bias[layer : layer + 1, i * part : (i + 1) * part] = matmul(ones, dense)[:1]
    send(bias, bias_hbm)
    for copy in copies:
        copy.wait()


VMEM = pl.BlockSpec(memory_space=pltpu.VMEM)
HBM = pl.BlockSpec(memory_space=pltpu.HBM)
MIB = 1024 * 1024


def call(kernel, ins, outs, scratch, *args, cost=None, room=24):
    args = [
        pltpu.with_memory_space_constraint(arg, pltpu.HBM) if spec is HBM else arg
        for spec, arg in zip(ins, args, strict=True)
    ]
    return pl.pallas_call(
        kernel,
        out_shape=tuple(
            (pltpu.HBM if spec is HBM else pltpu.VMEM)(shape, dtype) for shape, dtype, spec in outs
        ),
        in_specs=ins,
        out_specs=tuple(spec for _, _, spec in outs),
        scratch_shapes=scratch,
        cost_estimate=cost,
        compiler_params=pltpu.CompilerParams(vmem_limit_bytes=room * MIB),
    )(*args)


def share(value, axis):
    copies = jnp.broadcast_to(value[None], (lax.axis_size(axis),) + value.shape)
    return lax.all_to_all(copies, axis, 0, 0, tiled=True)


def by_pair(pairs, build, *args):
    branches = [functools.partial(build, pair) for pair in range(pairs)]
    if pairs == 1:
        return branches[0](*args)
    return lax.switch(lax.axis_index("layer") // FEAT_SPLIT, branches, *args)


def across(value, axis, step):
    pairs = [(i, i ^ step) for i in range(lax.axis_size(axis))]
    return lax.ppermute(value, axis, pairs)


def body(inputs, encoder, enc_bias, decoder, dec_bias, targets, top_index):
    tokens, layers, top_count = top_index.shape
    depth, width = encoder.shape[1:]
    feat = decoder.shape[3]
    slabs = lax.axis_size("lat")
    slab_most = 2 * top_count // slabs
    packed = tokens * layers * slab_most // LANES
    pairs = lax.axis_size("layer") // FEAT_SPLIT
    plan = (layers, width, top_count, slab_most)
    top = jnp.transpose(top_index, (1, 2, 0)).reshape(layers * top_count, tokens)
    dma = pltpu.SemaphoreType.DMA
    i16, i32 = jnp.int16, jnp.int32
    z, index, kept = call(
        functools.partial(encode_kernel, plan),
        [HBM] * 4,
        [
            ((packed, LANES), BF, VMEM),
            ((tokens, LANES), i16, VMEM),
            ((layers * slab_most, tokens), i32, VMEM),
        ],
        [
            pltpu.VMEM(inputs.shape, BF),
            pltpu.VMEM(encoder.shape, BF),
            pltpu.VMEM(enc_bias.shape, F32),
            pltpu.VMEM(top.shape, i32),
            pltpu.VMEM((layers, tokens, depth), BF),
            dma((4,)),
        ],
        inputs, encoder, enc_bias, top,
    )
    parts = share(z, "layer")
    (inverse,) = call(
        functools.partial(inverse_kernel, plan),
        [VMEM],
        [((layers, tokens, width), i16, VMEM)],
        [pltpu.VMEM((layers, 1 - (-width // (LANES * WORD_BLOCKS)), slab_most, tokens), i32)],
        kept,
        cost=pl.CostEstimate(flops=10**8, bytes_accessed=10**6, transcendentals=0),
    )

    def decode(pair, *args):
        return call(
            functools.partial(decode_kernel, plan, pair),
            [VMEM] * 4,
            [
                ((layers, tokens, width), BF, VMEM),
                ((2, tokens, feat), F32, VMEM),
                ((2, tokens, feat), BF, VMEM),
                ((tokens, LANES), i16, VMEM),
            ],
            [],
            *args,
        )

    act, mine, sent, index = by_pair(pairs, decode, parts, inverse, decoder[0], index)
    step = 1
    while 2 * step < slabs:
        mine = mine + across(sent, "lat", step).astype(F32)
        sent = mine.astype(BF)
        step *= 2
    sent, act = lax.optimization_barrier((sent, act))
    theirs = across(sent, "lat", step)
    act_t, x_t, targets_by_slot, decoder_t = call(
        turn_kernel,
        [VMEM] * 4,
        [
            ((layers, width, tokens), BF, VMEM),
            ((layers, depth, tokens), BF, VMEM),
            ((2, tokens, feat), BF, VMEM),
            ((layers + 1, feat, width), BF, VMEM),
        ],
        [],
        act, inputs, targets[0], decoder[0],
        cost=pl.CostEstimate(flops=10**8, bytes_accessed=10**7, transcendentals=0),
    )

    def residues(pair, *args):
        return call(
            functools.partial(residue_kernel, plan, pair),
            [VMEM] * 6,
            [((packed, LANES), BF, VMEM), ((2, tokens, feat), BF, VMEM)],
            [],
            *args,
        )

    z, residue = by_pair(
        pairs, residues, mine, theirs, dec_bias[0], targets_by_slot, index, decoder_t
    )
    parts = share(z, "layer")

    def grads(pair, *args):
        return call(
            functools.partial(grads_kernel, plan, pair),
            [VMEM] * 5,
            [
                ((layers + 1, width, feat), F32, HBM),
                (encoder.shape, F32, HBM),
                (enc_bias.shape, F32, HBM),
            ],
            [
                pltpu.VMEM((tokens, LANES), BF),
                pltpu.VMEM((layers + 1, width, feat), F32),
                pltpu.VMEM(encoder.shape, F32),
                pltpu.VMEM(enc_bias.shape, F32),
                dma((PARTS * (2 * layers + 1) + 1,)),
            ],
            *args,
        )

    decoder_grad, encoder_grad, bias_grad = by_pair(
        pairs, grads, parts, inverse, x_t, act_t, residue
    )
    return decoder_grad[None], encoder_grad, bias_grad


def solution(mesh):
    return jax.shard_map(
        body,
        mesh=mesh,
        in_specs=(
            P(None, None, "layer"),
            P(None, "layer", "lat"),
            P(None, "lat"),
            P("layer", None, "lat", None),
            P("layer", None, None),
            P("layer", None, None, None),
            P(),
        ),
        out_specs=(P("layer", None, "lat", None), P(None, "layer", "lat"), P(None, "lat")),
        check_vma=False,
    )
```

```python
import functools

import jax
import jax.numpy as jnp
from jax import lax
from jax.experimental import pallas as pl
from jax.experimental.pallas import tpu as pltpu
from jax.sharding import PartitionSpec as P

FEAT_SPLIT = 8
LANES = 128
PARTS = 4
CHUNK = 32
NUMBER_BITS = 7
WORD_BLOCKS = 31 // NUMBER_BITS

BF = jnp.bfloat16
F32 = jnp.float32
NT = (((1,), (1,)), ((), ()))
TN = (((0,), (0,)), ((), ()))


def matmul(left, right, dims=(((1,), (0,)), ((), ()))):
    return lax.dot_general(left, right, dims, preferred_element_type=F32)


def flag(condition):
    return jnp.where(condition, 1.0, 0.0).astype(BF)


def iota(shape, dimension):
    return lax.broadcasted_iota(jnp.int32, shape, dimension)


def pick_lanes(table, lanes):
    return lax.gather(
        table,
        lanes[..., None],
        lax.GatherDimensionNumbers(
            offset_dims=(),
            collapsed_slice_dims=(1,),
            start_index_map=(1,),
            operand_batching_dims=(0,),
            start_indices_batching_dims=(0,),
        ),
        slice_sizes=(1, 1),
        mode=lax.GatherScatterMode.PROMISE_IN_BOUNDS,
    )


def choose(options, index, bit):
    while len(options) > 1:
        odd = jnp.bitwise_and(index, jnp.int16(bit)) != 0
        options = [
            jnp.where(odd, options[i + 1], options[i]) if i + 1 < len(options) else options[i]
            for i in range(0, len(options), 2)
        ]
        bit *= 2
    return options[0]


def stride(width):
    return 1 << (width // LANES - 1).bit_length()


def gather_slots(dense, index):
    lane = jnp.bitwise_and(index, jnp.int16(LANES - 1))
    picked = [
        pick_lanes(dense[:, b * LANES : (b + 1) * LANES].astype(BF), lane)
        for b in range(dense.shape[1] // LANES)
    ]
    return choose(picked, index, LANES)


def join_layers(picked, index, width):
    total = choose(picked, index, LANES * stride(width))
    return jnp.where(index < 0, jnp.zeros_like(total), total).astype(F32)


def fold_slots(values, used):
    folds = LANES // used
    rows = values.shape[0] // folds
    total = values[:rows]
    for f in range(1, folds):
        total = total + pltpu.roll(values[f * rows : (f + 1) * rows], f * used, 1)
    return total


def sum_parts(parts_ref, used):
    total = jnp.sum(parts_ref[...].astype(F32), axis=0)
    folds = LANES // used
    total = jnp.concatenate(
        [pltpu.roll(total, (1 - f * used) % LANES, 1) for f in range(folds)], axis=0
    )
    lane = iota(total.shape, 1)
    return jnp.where((lane > 0) & (lane <= used), total, 0.0).astype(BF)


def place_slots(values, lane):
    blocks = lane.shape[1] // LANES
    return jnp.concatenate(
        [pick_lanes(values, lane[:, b * LANES : (b + 1) * LANES]) for b in range(blocks)],
        axis=1,
    )


def slot_index(top, slab, width, layers, top_count, slab_most):
    rows, tokens = top.shape
    place = jnp.bitwise_and(iota(top.shape, 0), top_count - 1)
    local = top - slab * width
    inside = (local >= 0) & (local < width)
    after = iota((rows, rows), 0)
    before = iota((rows, rows), 1)
    earlier = flag((before // top_count == after // top_count) & (before < after))
    rank = matmul(earlier, flag(inside)).astype(jnp.int32)
    local = local + (iota(top.shape, 0) // top_count) * (stride(width) * LANES)
    word = jnp.where(inside, (1 << 30) + ((place - rank) << 16) + local, 0)
    step = 0
    while (1 << step) < top_count:
        moved = pltpu.roll(word, rows - (1 << step), 0)
        bit = 1 << (16 + step)
        word = jnp.where((moved & bit) != 0, moved, jnp.where((word & bit) != 0, 0, word))
        step += 1
    index = jnp.where(word != 0, word & 0xFFFF, -1)
    return jnp.concatenate(
        [index[layer * top_count : layer * top_count + slab_most] for layer in range(layers)], axis=0
    )


def by_token(kept):
    spare = jnp.full((LANES - kept.shape[0], kept.shape[1]), -1, jnp.int32)
    return jnp.transpose(jnp.concatenate([kept, spare], axis=0), (1, 0))


def inverse_kernel(plan, kept_ref, inverse_ref, rows_ref):
    layers, width, top_count, slab_most = plan
    tokens = kept_ref.shape[1]
    blocks = width // LANES
    words = -(-blocks // WORD_BLOCKS)
    for layer in range(layers):
        own = kept_ref[layer * slab_most : (layer + 1) * slab_most, :]
        block = lax.shift_right_arithmetic(own, 7) - layer * stride(width)
        number = iota(own.shape, 0) + (1 + layer * slab_most)
        value = lax.shift_left(number, NUMBER_BITS * (block % WORD_BLOCKS))
        rows_ref[layer, 0] = jnp.bitwise_and(own, LANES - 1)
        for w in range(words):
            rows_ref[layer, 1 + w] = jnp.where((own >= 0) & (block // WORD_BLOCKS == w), value, 0)
        pieces = [[] for w in range(words)]
        for first in range(0, LANES, CHUNK):
            lane = iota((CHUNK, tokens), 0) + first
            totals = [jnp.zeros((CHUNK, tokens), jnp.int32) for w in range(words)]
            for s in range(slab_most):
                match = lane == rows_ref[layer, 0, s : s + 1, :]
                for w in range(words):
                    totals[w] = totals[w] + jnp.where(match, rows_ref[layer, 1 + w, s : s + 1, :], 0)
            for w in range(words):
                pieces[w].append(totals[w])
        for w in range(words):
            word = jnp.transpose(jnp.concatenate(pieces[w], axis=0), (1, 0))
            for b in range(w * WORD_BLOCKS, min((w + 1) * WORD_BLOCKS, blocks)):
                numbers = lax.shift_right_logical(word, NUMBER_BITS * (b % WORD_BLOCKS))
                inverse_ref[layer, :, b * LANES : (b + 1) * LANES] = jnp.bitwise_and(
                    numbers, LANES - 1
                ).astype(jnp.int16)


def encode_kernel(
    plan, x_hbm, encoder_hbm, bias_hbm, top_hbm, z_ref, index_ref, kept_ref,
    x_ref, encoder_ref, bias_ref, top_ref, x_layer, sems
):
    layers, width, top_count, slab_most = plan
    copies = [
        pltpu.make_async_copy(source, target, sems.at[i])
        for i, (source, target) in enumerate(
            [(top_hbm, top_ref), (x_hbm, x_ref), (bias_hbm, bias_ref), (encoder_hbm, encoder_ref)]
        )
    ]
    for copy in copies:
        copy.start()
    for copy in copies[:2]:
        copy.wait()
    tokens, depth = x_ref.shape[0], x_ref.shape[2]
    x_rows = x_ref[...].reshape(tokens * layers, depth)
    token, row = iota((tokens, tokens * layers), 0), iota((tokens, tokens * layers), 1)
    for layer in range(layers):
        x_layer[layer] = matmul(flag(row == layers * token + layer), x_rows).astype(BF)
    kept = slot_index(top_ref[...], lax.axis_index("lat"), width, layers, top_count, slab_most)
    kept_ref[...] = kept
    index = by_token(kept).astype(jnp.int16)
    index_ref[...] = index
    for copy in copies[2:]:
        copy.wait()
    with_bias = jnp.where(lax.axis_index("layer") == 0, 1.0, 0.0)
    picked = []
    for layer in range(layers):
        dense = matmul(x_layer[layer], encoder_ref[layer])
        dense = dense + bias_ref[layer : layer + 1, :] * with_bias
        picked.append(gather_slots(dense, index))
    z_ref[...] = fold_slots(join_layers(picked, index, width), layers * slab_most).astype(BF)


def block_places(layers, pair):
    return [(k, 0) if k <= pair else (k - pair - 1, 1) for k in range(layers + 1)]


def decode_kernel(
    plan, pair, parts_ref, inverse_ref, decoder_ref, index_ref,
    act_ref, first_ref, second_ref, first_rounded, second_rounded, index_out
):
    layers, width, top_count, slab_most = plan
    index_out[...] = index_ref[...]
    total = sum_parts(parts_ref, layers * slab_most)
    for layer in range(layers):
        act_ref[layer] = place_slots(total, inverse_ref[layer])
    sums = [None, None]
    for k, (source, slot) in enumerate(block_places(layers, pair)):
        term = matmul(act_ref[source], decoder_ref[k])
        sums[slot] = term if sums[slot] is None else sums[slot] + term
    first_ref[...] = sums[0]
    second_ref[...] = sums[1]
    first_rounded[...] = sums[0].astype(BF)
    second_rounded[...] = sums[1].astype(BF)


def turn_kernel(act_ref, x_ref, targets_ref, decoder_ref, act_t, x_t, targets_out, decoder_t):
    for layer in range(act_ref.shape[0]):
        act_t[layer] = jnp.transpose(act_ref[layer], (1, 0))
        x_t[layer] = jnp.transpose(x_ref[:, layer, :], (1, 0))
    for slot in range(2):
        targets_out[slot] = targets_ref[:, slot, :]
    for k in range(decoder_ref.shape[0]):
        decoder_t[k] = jnp.transpose(decoder_ref[k], (1, 0))


def residue_kernel(
    plan, pair, mine_a, mine_b, theirs_a, theirs_b, dec_bias_ref, targets_ref, index_ref, decoder_t,
    z_ref, residue
):
    layers, width, top_count, slab_most = plan
    for slot, (mine, theirs) in enumerate([(mine_a, theirs_a), (mine_b, theirs_b)]):
        rebuilt = mine[...] + theirs[...].astype(F32)
        rebuilt = rebuilt + dec_bias_ref[slot : slot + 1, :]
        residue[slot] = (rebuilt - targets_ref[slot].astype(F32)).astype(BF)
    places = block_places(layers, pair)
    index = index_ref[...]
    picked = []
    for layer in range(layers):
        dense = None
        for k, (source, slot) in enumerate(places):
            if source == layer:
                term = matmul(residue[slot], decoder_t[k])
                dense = term if dense is None else dense + term
        picked.append(jnp.zeros(index.shape, BF) if dense is None else gather_slots(dense, index))
    z_ref[...] = fold_slots(join_layers(picked, index, width), layers * slab_most).astype(BF)


def grads_kernel(
    plan, pair, parts_ref, inverse_ref, x_t, act_t, residue_ref,
    decoder_hbm, encoder_hbm, bias_hbm, values, decoder_grad, encoder_grad, bias, sems
):
    layers, width, top_count, slab_most = plan
    tokens = x_t.shape[2]
    part = width // PARTS
    copies = []

    def send(source, target):
        copies.append(pltpu.make_async_copy(source, target, sems.at[len(copies)]))
        copies[-1].start()

    for k, (source, slot) in enumerate(block_places(layers, pair)):
        for i in range(PARTS):
            rows = pl.ds(i * part, part)
            decoder_grad[k, rows] = matmul(act_t[source, rows], residue_ref[slot])
            send(decoder_grad.at[k, rows], decoder_hbm.at[k, rows])
    values[...] = sum_parts(parts_ref, layers * slab_most)
    ones = jnp.ones((8, tokens), BF)
    for layer in range(layers):
        for i in range(PARTS):
            at = (layer, slice(None), pl.ds(i * part, part))
            dense = place_slots(values[...], inverse_ref[at])
            encoder_grad[at] = matmul(x_t[layer], dense)
            send(encoder_grad.at[at], encoder_hbm.at[at])
            bias[layer : layer + 1, i * part : (i + 1) * part] = matmul(ones, dense)[:1]
    send(bias, bias_hbm)
    for copy in copies:
        copy.wait()


VMEM = pl.BlockSpec(memory_space=pltpu.VMEM)
HBM = pl.BlockSpec(memory_space=pltpu.HBM)
MIB = 1024 * 1024


def call(kernel, ins, outs, scratch, *args, cost=None, room=24):
    args = [
        pltpu.with_memory_space_constraint(arg, pltpu.HBM) if spec is HBM else arg
        for spec, arg in zip(ins, args, strict=True)
    ]
    return pl.pallas_call(
        kernel,
        out_shape=tuple(
            (pltpu.HBM if spec is HBM else pltpu.VMEM)(shape, dtype) for shape, dtype, spec in outs
        ),
        in_specs=ins,
        out_specs=tuple(spec for _, _, spec in outs),
        scratch_shapes=scratch,
        cost_estimate=cost,
        compiler_params=pltpu.CompilerParams(vmem_limit_bytes=room * MIB),
    )(*args)


def share(value, axis):
    copies = jnp.broadcast_to(value[None], (lax.axis_size(axis),) + value.shape)
    return lax.all_to_all(copies, axis, 0, 0, tiled=True)


def by_pair(pairs, build, *args):
    branches = [functools.partial(build, pair) for pair in range(pairs)]
    if pairs == 1:
        return branches[0](*args)
    return lax.switch(lax.axis_index("layer") // FEAT_SPLIT, branches, *args)


def across(value, axis, step):
    pairs = [(i, i ^ step) for i in range(lax.axis_size(axis))]
    return lax.ppermute(value, axis, pairs)


def body(inputs, encoder, enc_bias, decoder, dec_bias, targets, top_index):
    tokens, layers, top_count = top_index.shape
    depth, width = encoder.shape[1:]
    feat = decoder.shape[3]
    slabs = lax.axis_size("lat")
    slab_most = 2 * top_count // slabs
    packed = tokens * layers * slab_most // LANES
    pairs = lax.axis_size("layer") // FEAT_SPLIT
    plan = (layers, width, top_count, slab_most)
    top = jnp.transpose(top_index, (1, 2, 0)).reshape(layers * top_count, tokens)
    dma = pltpu.SemaphoreType.DMA
    i16, i32 = jnp.int16, jnp.int32
    z, index, kept = call(
        functools.partial(encode_kernel, plan),
        [HBM] * 4,
        [
            ((packed, LANES), BF, VMEM),
            ((tokens, LANES), i16, VMEM),
            ((layers * slab_most, tokens), i32, VMEM),
        ],
        [
            pltpu.VMEM(inputs.shape, BF),
            pltpu.VMEM(encoder.shape, BF),
            pltpu.VMEM(enc_bias.shape, F32),
            pltpu.VMEM(top.shape, i32),
            pltpu.VMEM((layers, tokens, depth), BF),
            dma((4,)),
        ],
        inputs, encoder, enc_bias, top,
    )
    parts = share(z, "layer")
    (inverse,) = call(
        functools.partial(inverse_kernel, plan),
        [VMEM],
        [((layers, tokens, width), i16, VMEM)],
        [pltpu.VMEM((layers, 1 - (-width // (LANES * WORD_BLOCKS)), slab_most, tokens), i32)],
        kept,
        cost=pl.CostEstimate(flops=10**8, bytes_accessed=10**6, transcendentals=0),
    )

    def decode(pair, *args):
        return call(
            functools.partial(decode_kernel, plan, pair),
            [VMEM] * 4,
            [
                ((layers, tokens, width), BF, VMEM),
                ((tokens, feat), F32, VMEM),
                ((tokens, feat), F32, VMEM),
                ((tokens, feat), BF, VMEM),
                ((tokens, feat), BF, VMEM),
                ((tokens, LANES), i16, VMEM),
            ],
            [],
            *args,
        )

    act, mine_a, mine_b, sent_a, sent_b, index = by_pair(
        pairs, decode, parts, inverse, decoder[0], index
    )
    steps = [1 << i for i in range(slabs.bit_length() - 1)]
    for i, step in enumerate(steps):
        theirs_a = across(sent_a, "lat", step)
        theirs_b = across(sent_b, "lat", steps[-1 - i])
        if i + 1 < len(steps):
            mine_a = mine_a + theirs_a.astype(F32)
            mine_b = mine_b + theirs_b.astype(F32)
            sent_a, sent_b = mine_a.astype(BF), mine_b.astype(BF)
            sent_a, act = lax.optimization_barrier((sent_a, act))
    act_t, x_t, targets_by_slot, decoder_t = call(
        turn_kernel,
        [VMEM] * 4,
        [
            ((layers, width, tokens), BF, VMEM),
            ((layers, depth, tokens), BF, VMEM),
            ((2, tokens, feat), BF, VMEM),
            ((layers + 1, feat, width), BF, VMEM),
        ],
        [],
        act, inputs, targets[0], decoder[0],
        cost=pl.CostEstimate(flops=10**8, bytes_accessed=10**7, transcendentals=0),
    )

    def residues(pair, *args):
        return call(
            functools.partial(residue_kernel, plan, pair),
            [VMEM] * 8,
            [((packed, LANES), BF, VMEM), ((2, tokens, feat), BF, VMEM)],
            [],
            *args,
        )

    z, residue = by_pair(
        pairs, residues, mine_a, mine_b, theirs_a, theirs_b, dec_bias[0], targets_by_slot, index, decoder_t
    )
    parts = share(z, "layer")

    def grads(pair, *args):
        return call(
            functools.partial(grads_kernel, plan, pair),
            [VMEM] * 5,
            [
                ((layers + 1, width, feat), F32, HBM),
                (encoder.shape, F32, HBM),
                (enc_bias.shape, F32, HBM),
            ],
            [
                pltpu.VMEM((tokens, LANES), BF),
                pltpu.VMEM((layers + 1, width, feat), F32),
                pltpu.VMEM(encoder.shape, F32),
                pltpu.VMEM(enc_bias.shape, F32),
                dma((PARTS * (2 * layers + 1) + 1,)),
            ],
            *args,
        )

    decoder_grad, encoder_grad, bias_grad = by_pair(
        pairs, grads, parts, inverse, x_t, act_t, residue
    )
    return decoder_grad[None], encoder_grad, bias_grad


def solution(mesh):
    return jax.shard_map(
        body,
        mesh=mesh,
        in_specs=(
            P(None, None, "layer"),
            P(None, "layer", "lat"),
            P(None, "lat"),
            P("layer", None, "lat", None),
            P("layer", None, None),
            P("layer", None, None, None),
            P(),
        ),
        out_specs=(P("layer", None, "lat", None), P(None, "layer", "lat"), P(None, "lat")),
        check_vma=False,
    )
```

```python
import functools

import jax
import jax.numpy as jnp
from jax import lax
from jax.experimental import pallas as pl
from jax.experimental.pallas import tpu as pltpu
from jax.sharding import PartitionSpec as P

FEAT_SPLIT = 8
LANES = 128
PARTS = 4
CHUNK = 32
NUMBER_BITS = 7
WORD_BLOCKS = 31 // NUMBER_BITS

BF = jnp.bfloat16
F32 = jnp.float32
NT = (((1,), (1,)), ((), ()))
TN = (((0,), (0,)), ((), ()))


def matmul(left, right, dims=(((1,), (0,)), ((), ()))):
    return lax.dot_general(left, right, dims, preferred_element_type=F32)


def flag(condition):
    return jnp.where(condition, 1.0, 0.0).astype(BF)


def iota(shape, dimension):
    return lax.broadcasted_iota(jnp.int32, shape, dimension)


def pick_lanes(table, lanes):
    return lax.gather(
        table,
        lanes[..., None],
        lax.GatherDimensionNumbers(
            offset_dims=(),
            collapsed_slice_dims=(1,),
            start_index_map=(1,),
            operand_batching_dims=(0,),
            start_indices_batching_dims=(0,),
        ),
        slice_sizes=(1, 1),
        mode=lax.GatherScatterMode.PROMISE_IN_BOUNDS,
    )


def choose(options, index, bit):
    while len(options) > 1:
        odd = jnp.bitwise_and(index, jnp.int16(bit)) != 0
        options = [
            jnp.where(odd, options[i + 1], options[i]) if i + 1 < len(options) else options[i]
            for i in range(0, len(options), 2)
        ]
        bit *= 2
    return options[0]


def stride(width):
    return 1 << (width // LANES - 1).bit_length()


def gather_slots(dense, index):
    lane = jnp.bitwise_and(index, jnp.int16(LANES - 1))
    picked = [
        pick_lanes(dense[:, b * LANES : (b + 1) * LANES].astype(BF), lane)
        for b in range(dense.shape[1] // LANES)
    ]
    return choose(picked, index, LANES)


def join_layers(picked, index, width):
    total = choose(picked, index, LANES * stride(width))
    return jnp.where(index < 0, jnp.zeros_like(total), total)


def fold_slots(values, used):
    rows = values.shape[0] * used // LANES
    total = values[:rows]
    for first in range(rows, values.shape[0], rows):
        total = total + values[first : first + rows]
    return total


def sum_parts(parts_ref, used):
    total = jnp.sum(parts_ref[...].astype(F32), axis=0)
    part = iota(total.shape, 1) // used
    return jnp.concatenate(
        [jnp.where(part == f, total, 0.0).astype(BF) for f in range(LANES // used)], axis=0
    )


def place_slots(values, lane):
    blocks = lane.shape[1] // LANES
    return jnp.concatenate(
        [pick_lanes(values, lane[:, b * LANES : (b + 1) * LANES]) for b in range(blocks)],
        axis=1,
    )


def slot_index(top, slab, width, layers, top_count, slab_most):
    rows, tokens = top.shape
    place = jnp.bitwise_and(iota(top.shape, 0), top_count - 1)
    local = top - slab * width
    inside = (local >= 0) & (local < width)
    after = iota((rows, rows), 0)
    before = iota((rows, rows), 1)
    earlier = flag((before // top_count == after // top_count) & (before < after))
    rank = matmul(earlier, flag(inside)).astype(jnp.int32)
    local = local + (iota(top.shape, 0) // top_count) * (stride(width) * LANES)
    word = jnp.where(inside, (1 << 30) + ((place - rank) << 16) + local, 0)
    step = 0
    while (1 << step) < top_count:
        moved = pltpu.roll(word, rows - (1 << step), 0)
        bit = 1 << (16 + step)
        word = jnp.where((moved & bit) != 0, moved, jnp.where((word & bit) != 0, 0, word))
        step += 1
    index = jnp.where(word != 0, word & 0xFFFF, -1)
    return jnp.concatenate(
        [index[layer * top_count : layer * top_count + slab_most] for layer in range(layers)], axis=0
    )


def by_token(kept):
    used, tokens = kept.shape
    folds = LANES // used
    part = iota(kept.shape, 1) // (tokens // folds)
    return jnp.transpose(
        jnp.concatenate([jnp.where(part == f, kept, -1) for f in range(folds)], axis=0), (1, 0)
    )


def inverse_kernel(plan, kept_ref, inverse_ref, rows_ref):
    layers, width, top_count, slab_most = plan
    tokens = kept_ref.shape[1]
    blocks = width // LANES
    words = -(-blocks // WORD_BLOCKS)
    used = layers * slab_most
    part = iota((tokens, LANES), 0) // (tokens * used // LANES)
    unused = (part + 1) % (LANES // used) * used
    for layer in range(layers):
        own = kept_ref[layer * slab_most : (layer + 1) * slab_most, :]
        block = lax.shift_right_arithmetic(own, 7) - layer * stride(width)
        number = iota(own.shape, 0) + (1 + layer * slab_most)
        value = lax.shift_left(number, NUMBER_BITS * (block % WORD_BLOCKS))
        rows_ref[layer, 0] = jnp.bitwise_and(own, LANES - 1)
        for w in range(words):
            rows_ref[layer, 1 + w] = jnp.where((own >= 0) & (block // WORD_BLOCKS == w), value, 0)
        pieces = [[] for w in range(words)]
        for first in range(0, LANES, CHUNK):
            lane = iota((CHUNK, tokens), 0) + first
            totals = [jnp.zeros((CHUNK, tokens), jnp.int32) for w in range(words)]
            for s in range(slab_most):
                match = lane == rows_ref[layer, 0, s : s + 1, :]
                for w in range(words):
                    totals[w] = totals[w] + jnp.where(match, rows_ref[layer, 1 + w, s : s + 1, :], 0)
            for w in range(words):
                pieces[w].append(totals[w])
        for w in range(words):
            word = jnp.transpose(jnp.concatenate(pieces[w], axis=0), (1, 0))
            for b in range(w * WORD_BLOCKS, min((w + 1) * WORD_BLOCKS, blocks)):
                numbers = lax.shift_right_logical(word, NUMBER_BITS * (b % WORD_BLOCKS))
                numbers = jnp.bitwise_and(numbers, LANES - 1)
                lanes = jnp.where(numbers > 0, numbers - 1 + part * used, unused)
                inverse_ref[layer, :, b * LANES : (b + 1) * LANES] = lanes.astype(jnp.int16)


def encode_kernel(
    plan, x_hbm, encoder_hbm, bias_hbm, top_hbm, z_ref, index_ref, kept_ref,
    x_ref, encoder_ref, bias_ref, top_ref, x_layer, sems
):
    layers, width, top_count, slab_most = plan
    copies = [
        pltpu.make_async_copy(source, target, sems.at[i])
        for i, (source, target) in enumerate(
            [(top_hbm, top_ref), (x_hbm, x_ref), (bias_hbm, bias_ref), (encoder_hbm, encoder_ref)]
        )
    ]
    for copy in copies:
        copy.start()
    for copy in copies[:2]:
        copy.wait()
    tokens, depth = x_ref.shape[0], x_ref.shape[2]
    x_rows = x_ref[...].reshape(tokens * layers, depth)
    token, row = iota((tokens, tokens * layers), 0), iota((tokens, tokens * layers), 1)
    for layer in range(layers):
        x_layer[layer] = matmul(flag(row == layers * token + layer), x_rows).astype(BF)
    kept = slot_index(top_ref[...], lax.axis_index("lat"), width, layers, top_count, slab_most)
    kept_ref[...] = kept
    index = by_token(kept).astype(jnp.int16)
    index_ref[...] = index
    for copy in copies[2:]:
        copy.wait()
    with_bias = jnp.where(lax.axis_index("layer") == 0, 1.0, 0.0)
    picked = []
    for layer in range(layers):
        dense = matmul(x_layer[layer], encoder_ref[layer])
        dense = dense + bias_ref[layer : layer + 1, :] * with_bias
        picked.append(gather_slots(dense, index))
    z_ref[...] = fold_slots(join_layers(picked, index, width), layers * slab_most)


def block_places(layers, pair):
    return [(k, 0) if k <= pair else (k - pair - 1, 1) for k in range(layers + 1)]


def decode_kernel(
    plan, pair, parts_ref, inverse_ref, decoder_ref, index_ref,
    act_ref, first_ref, second_ref, first_rounded, second_rounded, index_out
):
    layers, width, top_count, slab_most = plan
    index_out[...] = index_ref[...]
    total = sum_parts(parts_ref, layers * slab_most)
    for layer in range(layers):
        act_ref[layer] = place_slots(total, inverse_ref[layer])
    sums = [None, None]
    for k, (source, slot) in enumerate(block_places(layers, pair)):
        term = matmul(act_ref[source], decoder_ref[k])
        sums[slot] = term if sums[slot] is None else sums[slot] + term
    first_ref[...] = sums[0]
    second_ref[...] = sums[1]
    first_rounded[...] = sums[0].astype(BF)
    second_rounded[...] = sums[1].astype(BF)


def turn_kernel(act_ref, x_ref, targets_ref, decoder_ref, act_t, x_t, targets_out, decoder_t):
    for layer in range(act_ref.shape[0]):
        act_t[layer] = jnp.transpose(act_ref[layer], (1, 0))
        x_t[layer] = jnp.transpose(x_ref[:, layer, :], (1, 0))
    for slot in range(2):
        targets_out[slot] = targets_ref[:, slot, :]
    for k in range(decoder_ref.shape[0]):
        decoder_t[k] = jnp.transpose(decoder_ref[k], (1, 0))


def residue_kernel(
    plan, pair, mine_a, mine_b, theirs_a, theirs_b, dec_bias_ref, targets_ref, index_ref, decoder_t,
    z_ref, residue
):
    layers, width, top_count, slab_most = plan
    for slot, (mine, theirs) in enumerate([(mine_a, theirs_a), (mine_b, theirs_b)]):
        rebuilt = mine[...] + theirs[...].astype(F32)
        rebuilt = rebuilt + dec_bias_ref[slot : slot + 1, :]
        residue[slot] = (rebuilt - targets_ref[slot].astype(F32)).astype(BF)
    places = block_places(layers, pair)
    index = index_ref[...]
    picked = []
    for layer in range(layers):
        dense = None
        for k, (source, slot) in enumerate(places):
            if source == layer:
                term = matmul(residue[slot], decoder_t[k])
                dense = term if dense is None else dense + term
        picked.append(jnp.zeros(index.shape, BF) if dense is None else gather_slots(dense, index))
    z_ref[...] = fold_slots(join_layers(picked, index, width), layers * slab_most)


def grads_kernel(
    plan, pair, parts_ref, inverse_ref, x_t, act_t, residue_ref,
    decoder_hbm, encoder_hbm, bias_hbm, values, decoder_grad, encoder_grad, bias, sems
):
    layers, width, top_count, slab_most = plan
    tokens = x_t.shape[2]
    part = width // PARTS
    copies = []

    def send(source, target):
        copies.append(pltpu.make_async_copy(source, target, sems.at[len(copies)]))
        copies[-1].start()

    for k, (source, slot) in enumerate(block_places(layers, pair)):
        for i in range(PARTS):
            rows = pl.ds(i * part, part)
            decoder_grad[k, rows] = matmul(act_t[source, rows], residue_ref[slot])
            send(decoder_grad.at[k, rows], decoder_hbm.at[k, rows])
    values[...] = sum_parts(parts_ref, layers * slab_most)
    ones = jnp.ones((8, tokens), BF)
    for layer in range(layers):
        for i in range(PARTS):
            at = (layer, slice(None), pl.ds(i * part, part))
            dense = place_slots(values[...], inverse_ref[at])
            encoder_grad[at] = matmul(x_t[layer], dense)
            send(encoder_grad.at[at], encoder_hbm.at[at])
            bias[layer : layer + 1, i * part : (i + 1) * part] = matmul(ones, dense)[:1]
    send(bias, bias_hbm)
    for copy in copies:
        copy.wait()


VMEM = pl.BlockSpec(memory_space=pltpu.VMEM)
HBM = pl.BlockSpec(memory_space=pltpu.HBM)
MIB = 1024 * 1024


def call(kernel, ins, outs, scratch, *args, cost=None, room=24):
    args = [
        pltpu.with_memory_space_constraint(arg, pltpu.HBM) if spec is HBM else arg
        for spec, arg in zip(ins, args, strict=True)
    ]
    return pl.pallas_call(
        kernel,
        out_shape=tuple(
            (pltpu.HBM if spec is HBM else pltpu.VMEM)(shape, dtype) for shape, dtype, spec in outs
        ),
        in_specs=ins,
        out_specs=tuple(spec for _, _, spec in outs),
        scratch_shapes=scratch,
        cost_estimate=cost,
        compiler_params=pltpu.CompilerParams(vmem_limit_bytes=room * MIB),
    )(*args)


def share(value, axis):
    copies = jnp.broadcast_to(value[None], (lax.axis_size(axis),) + value.shape)
    return lax.all_to_all(copies, axis, 0, 0, tiled=True)


def by_pair(pairs, build, *args):
    branches = [functools.partial(build, pair) for pair in range(pairs)]
    if pairs == 1:
        return branches[0](*args)
    return lax.switch(lax.axis_index("layer") // FEAT_SPLIT, branches, *args)


def across(value, axis, step):
    pairs = [(i, i ^ step) for i in range(lax.axis_size(axis))]
    return lax.ppermute(value, axis, pairs)


def body(inputs, encoder, enc_bias, decoder, dec_bias, targets, top_index):
    tokens, layers, top_count = top_index.shape
    depth, width = encoder.shape[1:]
    feat = decoder.shape[3]
    slabs = lax.axis_size("lat")
    slab_most = 2 * top_count // slabs
    packed = tokens * layers * slab_most // LANES
    pairs = lax.axis_size("layer") // FEAT_SPLIT
    plan = (layers, width, top_count, slab_most)
    top = jnp.transpose(top_index, (1, 2, 0)).reshape(layers * top_count, tokens)
    dma = pltpu.SemaphoreType.DMA
    i16, i32 = jnp.int16, jnp.int32
    z, index, kept = call(
        functools.partial(encode_kernel, plan),
        [HBM] * 4,
        [
            ((packed, LANES), BF, VMEM),
            ((tokens, LANES), i16, VMEM),
            ((layers * slab_most, tokens), i32, VMEM),
        ],
        [
            pltpu.VMEM(inputs.shape, BF),
            pltpu.VMEM(encoder.shape, BF),
            pltpu.VMEM(enc_bias.shape, F32),
            pltpu.VMEM(top.shape, i32),
            pltpu.VMEM((layers, tokens, depth), BF),
            dma((4,)),
        ],
        inputs, encoder, enc_bias, top,
    )
    parts = share(z, "layer")
    (inverse,) = call(
        functools.partial(inverse_kernel, plan),
        [VMEM],
        [((layers, tokens, width), i16, VMEM)],
        [pltpu.VMEM((layers, 1 - (-width // (LANES * WORD_BLOCKS)), slab_most, tokens), i32)],
        kept,
        cost=pl.CostEstimate(flops=10**8, bytes_accessed=10**6, transcendentals=0),
    )

    def decode(pair, *args):
        return call(
            functools.partial(decode_kernel, plan, pair),
            [VMEM] * 4,
            [
                ((layers, tokens, width), BF, VMEM),
                ((tokens, feat), F32, VMEM),
                ((tokens, feat), F32, VMEM),
                ((tokens, feat), BF, VMEM),
                ((tokens, feat), BF, VMEM),
                ((tokens, LANES), i16, VMEM),
            ],
            [],
            *args,
        )

    act, mine_a, mine_b, sent_a, sent_b, index = by_pair(
        pairs, decode, parts, inverse, decoder[0], index
    )
    steps = [1 << i | 1 for i in range(slabs.bit_length() - 1)]
    for i, step in enumerate(steps):
        theirs_a = across(sent_a, "lat", step)
        theirs_b = across(sent_b, "lat", steps[-1 - i])
        if i + 1 < len(steps):
            mine_a = mine_a + theirs_a.astype(F32)
            mine_b = mine_b + theirs_b.astype(F32)
            sent_a, sent_b = mine_a.astype(BF), mine_b.astype(BF)
            sent_a, act = lax.optimization_barrier((sent_a, act))
    act_t, x_t, targets_by_slot, decoder_t = call(
        turn_kernel,
        [VMEM] * 4,
        [
            ((layers, width, tokens), BF, VMEM),
            ((layers, depth, tokens), BF, VMEM),
            ((2, tokens, feat), BF, VMEM),
            ((layers + 1, feat, width), BF, VMEM),
        ],
        [],
        act, inputs, targets[0], decoder[0],
        cost=pl.CostEstimate(flops=10**8, bytes_accessed=10**7, transcendentals=0),
    )

    def residues(pair, *args):
        return call(
            functools.partial(residue_kernel, plan, pair),
            [VMEM] * 8,
            [((packed, LANES), BF, VMEM), ((2, tokens, feat), BF, VMEM)],
            [],
            *args,
        )

    z, residue = by_pair(
        pairs, residues, mine_a, mine_b, theirs_a, theirs_b, dec_bias[0], targets_by_slot, index, decoder_t
    )
    parts = share(z, "layer")

    def grads(pair, *args):
        return call(
            functools.partial(grads_kernel, plan, pair),
            [VMEM] * 5,
            [
                ((layers + 1, width, feat), F32, HBM),
                (encoder.shape, F32, HBM),
                (enc_bias.shape, F32, HBM),
            ],
            [
                pltpu.VMEM((tokens, LANES), BF),
                pltpu.VMEM((layers + 1, width, feat), F32),
                pltpu.VMEM(encoder.shape, F32),
                pltpu.VMEM(enc_bias.shape, F32),
                dma((PARTS * (2 * layers + 1) + 1,)),
            ],
            *args,
        )

    decoder_grad, encoder_grad, bias_grad = by_pair(
        pairs, grads, parts, inverse, x_t, act_t, residue
    )
    return decoder_grad[None], encoder_grad, bias_grad


def solution(mesh):
    return jax.shard_map(
        body,
        mesh=mesh,
        in_specs=(
            P(None, None, "layer"),
            P(None, "layer", "lat"),
            P(None, "lat"),
            P("layer", None, "lat", None),
            P("layer", None, None),
            P("layer", None, None, None),
            P(),
        ),
        out_specs=(P("layer", None, "lat", None), P(None, "layer", "lat"), P(None, "lat")),
        check_vma=False,
    )
```

```python
import functools

import jax
import jax.numpy as jnp
from jax import lax
from jax.experimental import pallas as pl
from jax.experimental.pallas import tpu as pltpu
from jax.sharding import PartitionSpec as P

FEAT_SPLIT = 8
LANES = 128
PARTS = 4
CHUNK = 32
NUMBER_BITS = 7
WORD_BLOCKS = 31 // NUMBER_BITS

BF = jnp.bfloat16
F32 = jnp.float32
NT = (((1,), (1,)), ((), ()))
TN = (((0,), (0,)), ((), ()))


def matmul(left, right, dims=(((1,), (0,)), ((), ()))):
    return lax.dot_general(left, right, dims, preferred_element_type=F32)


def flag(condition):
    return jnp.where(condition, 1.0, 0.0).astype(BF)


def iota(shape, dimension):
    return lax.broadcasted_iota(jnp.int32, shape, dimension)


def pick_lanes(table, lanes):
    return lax.gather(
        table,
        lanes[..., None],
        lax.GatherDimensionNumbers(
            offset_dims=(),
            collapsed_slice_dims=(1,),
            start_index_map=(1,),
            operand_batching_dims=(0,),
            start_indices_batching_dims=(0,),
        ),
        slice_sizes=(1, 1),
        mode=lax.GatherScatterMode.PROMISE_IN_BOUNDS,
    )


def choose(options, index, bit):
    while len(options) > 1:
        odd = jnp.bitwise_and(index, jnp.int16(bit)) != 0
        options = [
            jnp.where(odd, options[i + 1], options[i]) if i + 1 < len(options) else options[i]
            for i in range(0, len(options), 2)
        ]
        bit *= 2
    return options[0]


def stride(width):
    return 1 << (width // LANES - 1).bit_length()


def gather_slots(dense, index):
    lane = jnp.bitwise_and(index, jnp.int16(LANES - 1))
    picked = [
        pick_lanes(dense[:, b * LANES : (b + 1) * LANES].astype(BF), lane)
        for b in range(dense.shape[1] // LANES)
    ]
    return choose(picked, index, LANES)


def join_layers(picked, index, width):
    total = choose(picked, index, LANES * stride(width))
    return jnp.where(index < 0, jnp.zeros_like(total), total)


def fold_slots(values, used):
    rows = values.shape[0] * used // LANES
    total = values[:rows]
    for first in range(rows, values.shape[0], rows):
        total = total + values[first : first + rows]
    return total


def sum_parts(parts_ref, used):
    total = jnp.sum(parts_ref[...].astype(F32), axis=0)
    part = iota(total.shape, 1) // used
    return jnp.concatenate(
        [jnp.where(part == f, total, 0.0).astype(BF) for f in range(LANES // used)], axis=0
    )


def place_slots(values, lane):
    blocks = lane.shape[1] // LANES
    return jnp.concatenate(
        [pick_lanes(values, lane[:, b * LANES : (b + 1) * LANES]) for b in range(blocks)],
        axis=1,
    )


def slot_index(top, slab, width, layers, top_count, slab_most):
    rows, tokens = top.shape
    place = jnp.bitwise_and(iota(top.shape, 0), top_count - 1)
    local = top - slab * width
    inside = (local >= 0) & (local < width)
    after = iota((rows, rows), 0)
    before = iota((rows, rows), 1)
    earlier = flag((before // top_count == after // top_count) & (before < after))
    rank = matmul(earlier, flag(inside)).astype(jnp.int32)
    local = local + (iota(top.shape, 0) // top_count) * (stride(width) * LANES)
    word = jnp.where(inside, (1 << 30) + ((place - rank) << 16) + local, 0)
    step = 0
    while (1 << step) < top_count:
        moved = pltpu.roll(word, rows - (1 << step), 0)
        bit = 1 << (16 + step)
        word = jnp.where((moved & bit) != 0, moved, jnp.where((word & bit) != 0, 0, word))
        step += 1
    index = jnp.where(word != 0, word & 0xFFFF, -1)
    return jnp.concatenate(
        [index[layer * top_count : layer * top_count + slab_most] for layer in range(layers)], axis=0
    )


def by_token(kept):
    used, tokens = kept.shape
    folds = LANES // used
    part = iota(kept.shape, 1) // (tokens // folds)
    return jnp.transpose(
        jnp.concatenate([jnp.where(part == f, kept, -1) for f in range(folds)], axis=0), (1, 0)
    )


def inverse_kernel(plan, kept_ref, inverse_ref, rows_ref):
    layers, width, top_count, slab_most = plan
    tokens = kept_ref.shape[1]
    blocks = width // LANES
    words = -(-blocks // WORD_BLOCKS)
    used = layers * slab_most
    part = iota((tokens, LANES), 0) // (tokens * used // LANES)
    unused = (part + 1) % (LANES // used) * used
    for layer in range(layers):
        own = kept_ref[layer * slab_most : (layer + 1) * slab_most, :]
        block = lax.shift_right_arithmetic(own, 7) - layer * stride(width)
        number = iota(own.shape, 0) + (1 + layer * slab_most)
        value = lax.shift_left(number, NUMBER_BITS * (block % WORD_BLOCKS))
        rows_ref[layer, 0] = jnp.bitwise_and(own, LANES - 1)
        for w in range(words):
            rows_ref[layer, 1 + w] = jnp.where((own >= 0) & (block // WORD_BLOCKS == w), value, 0)
        pieces = [[] for w in range(words)]
        for first in range(0, LANES, CHUNK):
            lane = iota((CHUNK, tokens), 0) + first
            totals = [jnp.zeros((CHUNK, tokens), jnp.int32) for w in range(words)]
            for s in range(slab_most):
                match = lane == rows_ref[layer, 0, s : s + 1, :]
                for w in range(words):
                    totals[w] = totals[w] + jnp.where(match, rows_ref[layer, 1 + w, s : s + 1, :], 0)
            for w in range(words):
                pieces[w].append(totals[w])
        for w in range(words):
            word = jnp.transpose(jnp.concatenate(pieces[w], axis=0), (1, 0))
            for b in range(w * WORD_BLOCKS, min((w + 1) * WORD_BLOCKS, blocks)):
                numbers = lax.shift_right_logical(word, NUMBER_BITS * (b % WORD_BLOCKS))
                numbers = jnp.bitwise_and(numbers, LANES - 1)
                lanes = jnp.where(numbers > 0, numbers - 1 + part * used, unused)
                inverse_ref[layer, :, b * LANES : (b + 1) * LANES] = lanes.astype(jnp.int16)


def encode_kernel(
    plan, x_hbm, encoder_hbm, bias_hbm, top_hbm, z_ref, index_ref, kept_ref,
    x_ref, encoder_ref, bias_ref, top_ref, x_layer, sems
):
    layers, width, top_count, slab_most = plan
    copies = [
        pltpu.make_async_copy(source, target, sems.at[i])
        for i, (source, target) in enumerate(
            [(top_hbm, top_ref), (x_hbm, x_ref), (bias_hbm, bias_ref), (encoder_hbm, encoder_ref)]
        )
    ]
    for copy in copies:
        copy.start()
    for copy in copies[:2]:
        copy.wait()
    tokens, depth = x_ref.shape[0], x_ref.shape[2]
    x_rows = x_ref[...].reshape(tokens * layers, depth)
    token, row = iota((tokens, tokens * layers), 0), iota((tokens, tokens * layers), 1)
    for layer in range(layers):
        x_layer[layer] = matmul(flag(row == layers * token + layer), x_rows).astype(BF)
    kept = slot_index(top_ref[...], lax.axis_index("lat"), width, layers, top_count, slab_most)
    kept_ref[...] = kept
    index = by_token(kept).astype(jnp.int16)
    index_ref[...] = index
    for copy in copies[2:]:
        copy.wait()
    with_bias = jnp.where(lax.axis_index("layer") == 0, 1.0, 0.0)
    picked = []
    for layer in range(layers):
        dense = matmul(x_layer[layer], encoder_ref[layer])
        dense = dense + bias_ref[layer : layer + 1, :] * with_bias
        picked.append(gather_slots(dense, index))
    z_ref[...] = fold_slots(join_layers(picked, index, width), layers * slab_most)


def block_places(layers, pair):
    return [(k, 0) if k <= pair else (k - pair - 1, 1) for k in range(layers + 1)]


def decode_kernel(
    plan, pair, parts_ref, inverse_ref, decoder_ref, index_ref,
    act_ref, first_ref, second_ref, first_rounded, second_rounded, index_out
):
    layers, width, top_count, slab_most = plan
    index_out[...] = index_ref[...]
    total = sum_parts(parts_ref, layers * slab_most)
    for layer in range(layers):
        act_ref[layer] = place_slots(total, inverse_ref[layer])
    sums = [None, None]
    for k, (source, slot) in enumerate(block_places(layers, pair)):
        term = matmul(act_ref[source], decoder_ref[k])
        sums[slot] = term if sums[slot] is None else sums[slot] + term
    first_ref[...] = sums[0]
    second_ref[...] = sums[1]
    first_rounded[...] = sums[0].astype(BF)
    second_rounded[...] = sums[1].astype(BF)


def turn_kernel(act_ref, x_ref, targets_ref, decoder_ref, act_t, x_t, targets_out, decoder_t):
    for layer in range(act_ref.shape[0]):
        act_t[layer] = jnp.transpose(act_ref[layer], (1, 0))
        x_t[layer] = jnp.transpose(x_ref[:, layer, :], (1, 0))
    for slot in range(2):
        targets_out[slot] = targets_ref[:, slot, :]
    for k in range(decoder_ref.shape[0]):
        decoder_t[k] = jnp.transpose(decoder_ref[k], (1, 0))


def residue_kernel(
    plan, pair, mine_a, mine_b, theirs_a, theirs_b, dec_bias_ref, targets_ref, index_ref, decoder_t,
    act_t, z_ref, residue, head_ref
):
    layers, width, top_count, slab_most = plan
    for slot, (mine, theirs) in enumerate([(mine_a, theirs_a), (mine_b, theirs_b)]):
        rebuilt = mine[...] + theirs[...].astype(F32)
        rebuilt = rebuilt + dec_bias_ref[slot : slot + 1, :]
        residue[slot] = (rebuilt - targets_ref[slot].astype(F32)).astype(BF)
    places = block_places(layers, pair)
    index = index_ref[...]
    picked = []
    for layer in range(layers):
        dense = None
        for k, (source, slot) in enumerate(places):
            if source == layer:
                term = matmul(residue[slot], decoder_t[k])
                dense = term if dense is None else dense + term
        picked.append(jnp.zeros(index.shape, BF) if dense is None else gather_slots(dense, index))
    z_ref[...] = fold_slots(join_layers(picked, index, width), layers * slab_most)
    head_ref[...] = matmul(act_t[places[0][0]], residue[places[0][1]])


def grads_kernel(
    plan, pair, parts_ref, inverse_ref, x_t, act_t, residue_ref, head_ref,
    decoder_hbm, encoder_hbm, bias_hbm, values, decoder_grad, encoder_grad, bias, sems
):
    layers, width, top_count, slab_most = plan
    tokens = x_t.shape[2]
    part = width // PARTS
    copies = []

    def send(source, target):
        copies.append(pltpu.make_async_copy(source, target, sems.at[len(copies)]))
        copies[-1].start()

    send(head_ref, decoder_hbm.at[0])
    values[...] = sum_parts(parts_ref, layers * slab_most)
    ones = jnp.ones((8, tokens), BF)
    for layer in range(layers):
        for i in range(PARTS):
            at = (layer, slice(None), pl.ds(i * part, part))
            dense = place_slots(values[...], inverse_ref[at])
            encoder_grad[at] = matmul(x_t[layer], dense)
            send(encoder_grad.at[at], encoder_hbm.at[at])
            bias[layer : layer + 1, i * part : (i + 1) * part] = matmul(ones, dense)[:1]
    for k, (source, slot) in list(enumerate(block_places(layers, pair)))[1:]:
        for i in range(PARTS):
            rows = pl.ds(i * part, part)
            decoder_grad[k - 1, rows] = matmul(act_t[source, rows], residue_ref[slot])
            send(decoder_grad.at[k - 1, rows], decoder_hbm.at[k, rows])
    send(bias, bias_hbm)
    for copy in copies:
        copy.wait()


VMEM = pl.BlockSpec(memory_space=pltpu.VMEM)
HBM = pl.BlockSpec(memory_space=pltpu.HBM)
MIB = 1024 * 1024


def call(kernel, ins, outs, scratch, *args, cost=None, room=24):
    args = [
        pltpu.with_memory_space_constraint(arg, pltpu.HBM) if spec is HBM else arg
        for spec, arg in zip(ins, args, strict=True)
    ]
    return pl.pallas_call(
        kernel,
        out_shape=tuple(
            (pltpu.HBM if spec is HBM else pltpu.VMEM)(shape, dtype) for shape, dtype, spec in outs
        ),
        in_specs=ins,
        out_specs=tuple(spec for _, _, spec in outs),
        scratch_shapes=scratch,
        cost_estimate=cost,
        compiler_params=pltpu.CompilerParams(vmem_limit_bytes=room * MIB),
    )(*args)


def share(value, axis):
    copies = jnp.broadcast_to(value[None], (lax.axis_size(axis),) + value.shape)
    return lax.all_to_all(copies, axis, 0, 0, tiled=True)


def by_pair(pairs, build, *args):
    branches = [functools.partial(build, pair) for pair in range(pairs)]
    if pairs == 1:
        return branches[0](*args)
    return lax.switch(lax.axis_index("layer") // FEAT_SPLIT, branches, *args)


def across(value, axis, step):
    pairs = [(i, i ^ step) for i in range(lax.axis_size(axis))]
    return lax.ppermute(value, axis, pairs)


def body(inputs, encoder, enc_bias, decoder, dec_bias, targets, top_index):
    tokens, layers, top_count = top_index.shape
    depth, width = encoder.shape[1:]
    feat = decoder.shape[3]
    slabs = lax.axis_size("lat")
    slab_most = 2 * top_count // slabs
    packed = tokens * layers * slab_most // LANES
    pairs = lax.axis_size("layer") // FEAT_SPLIT
    plan = (layers, width, top_count, slab_most)
    top = jnp.transpose(top_index, (1, 2, 0)).reshape(layers * top_count, tokens)
    dma = pltpu.SemaphoreType.DMA
    i16, i32 = jnp.int16, jnp.int32
    z, index, kept = call(
        functools.partial(encode_kernel, plan),
        [HBM] * 4,
        [
            ((packed, LANES), BF, VMEM),
            ((tokens, LANES), i16, VMEM),
            ((layers * slab_most, tokens), i32, VMEM),
        ],
        [
            pltpu.VMEM(inputs.shape, BF),
            pltpu.VMEM(encoder.shape, BF),
            pltpu.VMEM(enc_bias.shape, F32),
            pltpu.VMEM(top.shape, i32),
            pltpu.VMEM((layers, tokens, depth), BF),
            dma((4,)),
        ],
        inputs, encoder, enc_bias, top,
    )
    parts = share(z, "layer")
    (inverse,) = call(
        functools.partial(inverse_kernel, plan),
        [VMEM],
        [((layers, tokens, width), i16, VMEM)],
        [pltpu.VMEM((layers, 1 - (-width // (LANES * WORD_BLOCKS)), slab_most, tokens), i32)],
        kept,
        cost=pl.CostEstimate(flops=10**8, bytes_accessed=10**6, transcendentals=0),
    )

    def decode(pair, *args):
        return call(
            functools.partial(decode_kernel, plan, pair),
            [VMEM] * 4,
            [
                ((layers, tokens, width), BF, VMEM),
                ((tokens, feat), F32, VMEM),
                ((tokens, feat), F32, VMEM),
                ((tokens, feat), BF, VMEM),
                ((tokens, feat), BF, VMEM),
                ((tokens, LANES), i16, VMEM),
            ],
            [],
            *args,
        )

    act, mine_a, mine_b, sent_a, sent_b, index = by_pair(
        pairs, decode, parts, inverse, decoder[0], index
    )
    steps = [1 << i | 1 for i in range(slabs.bit_length() - 1)]
    for i in range(len(steps)):
        theirs_a = across(sent_a, "lat", 1 << i)
        theirs_b = across(sent_b, "lat", steps[-1 - i])
        if i + 1 < len(steps):
            mine_a = mine_a + theirs_a.astype(F32)
            mine_b = mine_b + theirs_b.astype(F32)
            sent_a, sent_b = mine_a.astype(BF), mine_b.astype(BF)
            sent_a, act = lax.optimization_barrier((sent_a, act))
    act_t, x_t, targets_by_slot, decoder_t = call(
        turn_kernel,
        [VMEM] * 4,
        [
            ((layers, width, tokens), BF, VMEM),
            ((layers, depth, tokens), BF, VMEM),
            ((2, tokens, feat), BF, VMEM),
            ((layers + 1, feat, width), BF, VMEM),
        ],
        [],
        act, inputs, targets[0], decoder[0],
        cost=pl.CostEstimate(flops=10**8, bytes_accessed=10**7, transcendentals=0),
    )

    def residues(pair, *args):
        return call(
            functools.partial(residue_kernel, plan, pair),
            [VMEM] * 9,
            [
                ((packed, LANES), BF, VMEM),
                ((2, tokens, feat), BF, VMEM),
                ((width, feat), F32, VMEM),
            ],
            [],
            *args,
        )

    z, residue, head = by_pair(
        pairs, residues, mine_a, mine_b, theirs_a, theirs_b, dec_bias[0], targets_by_slot, index, decoder_t, act_t
    )
    parts = share(z, "layer")

    def grads(pair, *args):
        return call(
            functools.partial(grads_kernel, plan, pair),
            [VMEM] * 6,
            [
                ((layers + 1, width, feat), F32, HBM),
                (encoder.shape, F32, HBM),
                (enc_bias.shape, F32, HBM),
            ],
            [
                pltpu.VMEM((tokens, LANES), BF),
                pltpu.VMEM((layers, width, feat), F32),
                pltpu.VMEM(encoder.shape, F32),
                pltpu.VMEM(enc_bias.shape, F32),
                dma((PARTS * 2 * layers + 2,)),
            ],
            *args,
        )

    decoder_grad, encoder_grad, bias_grad = by_pair(
        pairs, grads, parts, inverse, x_t, act_t, residue, head
    )
    return decoder_grad[None], encoder_grad, bias_grad


def solution(mesh):
    return jax.shard_map(
        body,
        mesh=mesh,
        in_specs=(
            P(None, None, "layer"),
            P(None, "layer", "lat"),
            P(None, "lat"),
            P("layer", None, "lat", None),
            P("layer", None, None),
            P("layer", None, None, None),
            P(),
        ),
        out_specs=(P("layer", None, "lat", None), P(None, "layer", "lat"), P(None, "lat")),
        check_vma=False,
    )
```

```python
import functools

import jax
import jax.numpy as jnp
from jax import lax
from jax.experimental import pallas as pl
from jax.experimental.pallas import tpu as pltpu
from jax.sharding import PartitionSpec as P

FEAT_SPLIT = 8
LANES = 128
PARTS = 4
CHUNK = 32
NUMBER_BITS = 7
WORD_BLOCKS = 31 // NUMBER_BITS

BF = jnp.bfloat16
F32 = jnp.float32
NT = (((1,), (1,)), ((), ()))
TN = (((0,), (0,)), ((), ()))


def matmul(left, right, dims=(((1,), (0,)), ((), ()))):
    return lax.dot_general(left, right, dims, preferred_element_type=F32)


def flag(condition):
    return jnp.where(condition, 1.0, 0.0).astype(BF)


def iota(shape, dimension):
    return lax.broadcasted_iota(jnp.int32, shape, dimension)


def pick_lanes(table, lanes):
    return lax.gather(
        table,
        lanes[..., None],
        lax.GatherDimensionNumbers(
            offset_dims=(),
            collapsed_slice_dims=(1,),
            start_index_map=(1,),
            operand_batching_dims=(0,),
            start_indices_batching_dims=(0,),
        ),
        slice_sizes=(1, 1),
        mode=lax.GatherScatterMode.PROMISE_IN_BOUNDS,
    )


def choose(options, index, bit):
    while len(options) > 1:
        odd = jnp.bitwise_and(index, jnp.int16(bit)) != 0
        options = [
            jnp.where(odd, options[i + 1], options[i]) if i + 1 < len(options) else options[i]
            for i in range(0, len(options), 2)
        ]
        bit *= 2
    return options[0]


def stride(width):
    return 1 << (width // LANES - 1).bit_length()


def gather_slots(dense, index):
    lane = jnp.bitwise_and(index, jnp.int16(LANES - 1))
    picked = [
        pick_lanes(dense[:, b * LANES : (b + 1) * LANES].astype(BF), lane)
        for b in range(dense.shape[1] // LANES)
    ]
    return choose(picked, index, LANES)


def join_layers(picked, index, width):
    total = choose(picked, index, LANES * stride(width))
    return jnp.where(index < 0, jnp.zeros_like(total), total)


def fold_slots(values, used):
    rows = values.shape[0] * used // LANES
    total = values[:rows]
    for first in range(rows, values.shape[0], rows):
        total = total + values[first : first + rows]
    return total


def sum_parts(parts_ref, used):
    total = jnp.sum(parts_ref[...].astype(F32), axis=0)
    part = iota(total.shape, 1) // used
    return jnp.concatenate(
        [jnp.where(part == f, total, 0.0).astype(BF) for f in range(LANES // used)], axis=0
    )


def place_slots(values, lane):
    blocks = lane.shape[1] // LANES
    return jnp.concatenate(
        [pick_lanes(values, lane[:, b * LANES : (b + 1) * LANES]) for b in range(blocks)],
        axis=1,
    )


def slot_index(top, slab, width, layers, top_count, slab_most):
    rows, tokens = top.shape
    place = jnp.bitwise_and(iota(top.shape, 0), top_count - 1)
    local = top - slab * width
    inside = (local >= 0) & (local < width)
    after = iota((rows, rows), 0)
    before = iota((rows, rows), 1)
    earlier = flag((before // top_count == after // top_count) & (before < after))
    rank = matmul(earlier, flag(inside)).astype(jnp.int32)
    local = local + (iota(top.shape, 0) // top_count) * (stride(width) * LANES)
    word = jnp.where(inside, (1 << 30) + ((place - rank) << 16) + local, 0)
    step = 0
    while (1 << step) < top_count:
        moved = pltpu.roll(word, rows - (1 << step), 0)
        bit = 1 << (16 + step)
        word = jnp.where((moved & bit) != 0, moved, jnp.where((word & bit) != 0, 0, word))
        step += 1
    index = jnp.where(word != 0, word & 0xFFFF, -1)
    return jnp.concatenate(
        [index[layer * top_count : layer * top_count + slab_most] for layer in range(layers)], axis=0
    )


def by_token(kept):
    used, tokens = kept.shape
    folds = LANES // used
    part = iota(kept.shape, 1) // (tokens // folds)
    return jnp.transpose(
        jnp.concatenate([jnp.where(part == f, kept, -1) for f in range(folds)], axis=0), (1, 0)
    )


def inverse_kernel(plan, kept_ref, inverse_ref, rows_ref):
    layers, width, top_count, slab_most = plan
    tokens = kept_ref.shape[1]
    blocks = width // LANES
    words = -(-blocks // WORD_BLOCKS)
    used = layers * slab_most
    part = iota((tokens, LANES), 0) // (tokens * used // LANES)
    unused = (part + 1) % (LANES // used) * used
    for layer in range(layers):
        own = kept_ref[layer * slab_most : (layer + 1) * slab_most, :]
        block = lax.shift_right_arithmetic(own, 7) - layer * stride(width)
        number = iota(own.shape, 0) + (1 + layer * slab_most)
        value = lax.shift_left(number, NUMBER_BITS * (block % WORD_BLOCKS))
        rows_ref[layer, 0] = jnp.bitwise_and(own, LANES - 1)
        for w in range(words):
            rows_ref[layer, 1 + w] = jnp.where((own >= 0) & (block // WORD_BLOCKS == w), value, 0)
        pieces = [[] for w in range(words)]
        for first in range(0, LANES, CHUNK):
            lane = iota((CHUNK, tokens), 0) + first
            totals = [jnp.zeros((CHUNK, tokens), jnp.int32) for w in range(words)]
            for s in range(slab_most):
                match = lane == rows_ref[layer, 0, s : s + 1, :]
                for w in range(words):
                    totals[w] = totals[w] + jnp.where(match, rows_ref[layer, 1 + w, s : s + 1, :], 0)
            for w in range(words):
                pieces[w].append(totals[w])
        for w in range(words):
            word = jnp.transpose(jnp.concatenate(pieces[w], axis=0), (1, 0))
            for b in range(w * WORD_BLOCKS, min((w + 1) * WORD_BLOCKS, blocks)):
                numbers = lax.shift_right_logical(word, NUMBER_BITS * (b % WORD_BLOCKS))
                numbers = jnp.bitwise_and(numbers, LANES - 1)
                lanes = jnp.where(numbers > 0, numbers - 1 + part * used, unused)
                inverse_ref[layer, :, b * LANES : (b + 1) * LANES] = lanes.astype(jnp.int16)


def encode_kernel(
    plan, x_hbm, encoder_hbm, bias_hbm, top_hbm, z_ref, index_ref, kept_ref,
    x_ref, encoder_ref, bias_ref, top_ref, x_layer, sems
):
    layers, width, top_count, slab_most = plan
    copies = [
        pltpu.make_async_copy(source, target, sems.at[i])
        for i, (source, target) in enumerate(
            [(top_hbm, top_ref), (x_hbm, x_ref), (bias_hbm, bias_ref), (encoder_hbm, encoder_ref)]
        )
    ]
    for copy in copies:
        copy.start()
    for copy in copies[:2]:
        copy.wait()
    tokens, depth = x_ref.shape[0], x_ref.shape[2]
    x_rows = x_ref[...].reshape(tokens * layers, depth)
    token, row = iota((tokens, tokens * layers), 0), iota((tokens, tokens * layers), 1)
    for layer in range(layers):
        x_layer[layer] = matmul(flag(row == layers * token + layer), x_rows).astype(BF)
    kept = slot_index(top_ref[...], lax.axis_index("lat"), width, layers, top_count, slab_most)
    kept_ref[...] = kept
    index = by_token(kept).astype(jnp.int16)
    index_ref[...] = index
    for copy in copies[2:]:
        copy.wait()
    with_bias = jnp.where(lax.axis_index("layer") == 0, 1.0, 0.0)
    picked = []
    for layer in range(layers):
        dense = matmul(x_layer[layer], encoder_ref[layer])
        dense = dense + bias_ref[layer : layer + 1, :] * with_bias
        picked.append(gather_slots(dense, index))
    z_ref[...] = fold_slots(join_layers(picked, index, width), layers * slab_most)


def block_places(layers, pair):
    return [(k, 0) if k <= pair else (k - pair - 1, 1) for k in range(layers + 1)]


def decode_kernel(
    plan, pair, parts_ref, inverse_ref, decoder_ref, index_ref,
    act_ref, first_ref, second_ref, first_rounded, second_rounded, index_out
):
    layers, width, top_count, slab_most = plan
    index_out[...] = index_ref[...]
    total = sum_parts(parts_ref, layers * slab_most)
    for layer in range(layers):
        act_ref[layer] = place_slots(total, inverse_ref[layer])
    sums = [None, None]
    for k, (source, slot) in enumerate(block_places(layers, pair)):
        term = matmul(act_ref[source], decoder_ref[k])
        sums[slot] = term if sums[slot] is None else sums[slot] + term
    first_ref[...] = sums[0]
    second_ref[...] = sums[1]
    first_rounded[...] = sums[0].astype(BF)
    second_rounded[...] = sums[1].astype(BF)


def turn_kernel(act_ref, x_ref, targets_ref, decoder_ref, act_t, x_t, targets_out, decoder_t):
    for layer in range(act_ref.shape[0]):
        act_t[layer] = jnp.transpose(act_ref[layer], (1, 0))
        x_t[layer] = jnp.transpose(x_ref[:, layer, :], (1, 0))
    for slot in range(2):
        targets_out[slot] = targets_ref[:, slot, :]
    for k in range(decoder_ref.shape[0]):
        decoder_t[k] = jnp.transpose(decoder_ref[k], (1, 0))


def residue_kernel(
    plan, pair, mine_a, mine_b, theirs_a, theirs_b, dec_bias_ref, targets_ref, index_ref, decoder_t,
    act_t, z_ref, residue, head_ref
):
    layers, width, top_count, slab_most = plan
    for slot, (mine, theirs) in enumerate([(mine_a, theirs_a), (mine_b, theirs_b)]):
        rebuilt = mine[...] + theirs[...].astype(F32)
        rebuilt = rebuilt + dec_bias_ref[slot : slot + 1, :]
        residue[slot] = (rebuilt - targets_ref[slot].astype(F32)).astype(BF)
    places = block_places(layers, pair)
    index = index_ref[...]
    picked = []
    for layer in range(layers):
        dense = None
        for k, (source, slot) in enumerate(places):
            if source == layer:
                term = matmul(residue[slot], decoder_t[k])
                dense = term if dense is None else dense + term
        picked.append(jnp.zeros(index.shape, BF) if dense is None else gather_slots(dense, index))
    z_ref[...] = fold_slots(join_layers(picked, index, width), layers * slab_most)
    head_ref[...] = matmul(act_t[places[0][0]], residue[places[0][1]])


def grads_kernel(
    plan, pair, parts_ref, inverse_ref, x_t, act_t, residue_ref, head_ref,
    decoder_hbm, encoder_hbm, bias_hbm, values, decoder_grad, encoder_grad, bias, sems
):
    layers, width, top_count, slab_most = plan
    tokens = x_t.shape[2]
    part = width // PARTS
    copies = []

    def send(source, target):
        copies.append(pltpu.make_async_copy(source, target, sems.at[len(copies)]))
        copies[-1].start()

    send(head_ref, decoder_hbm.at[0])
    values[...] = sum_parts(parts_ref, layers * slab_most)
    ones = jnp.ones((8, tokens), BF)
    for layer in range(layers):
        for i in range(PARTS):
            at = (layer, slice(None), pl.ds(i * part, part))
            dense = place_slots(values[...], inverse_ref[at])
            encoder_grad[at] = matmul(x_t[layer], dense)
            send(encoder_grad.at[at], encoder_hbm.at[at])
            bias[layer : layer + 1, i * part : (i + 1) * part] = matmul(ones, dense)[:1]
    for k, (source, slot) in list(enumerate(block_places(layers, pair)))[1:]:
        for i in range(PARTS):
            rows = pl.ds(i * part, part)
            decoder_grad[k - 1, rows] = matmul(act_t[source, rows], residue_ref[slot])
            send(decoder_grad.at[k - 1, rows], decoder_hbm.at[k, rows])
    send(bias, bias_hbm)
    for copy in copies:
        copy.wait()


VMEM = pl.BlockSpec(memory_space=pltpu.VMEM)
HBM = pl.BlockSpec(memory_space=pltpu.HBM)
MIB = 1024 * 1024


def call(kernel, ins, outs, scratch, *args, cost=None, room=24):
    args = [
        pltpu.with_memory_space_constraint(arg, pltpu.HBM) if spec is HBM else arg
        for spec, arg in zip(ins, args, strict=True)
    ]
    return pl.pallas_call(
        kernel,
        out_shape=tuple(
            (pltpu.HBM if spec is HBM else pltpu.VMEM)(shape, dtype) for shape, dtype, spec in outs
        ),
        in_specs=ins,
        out_specs=tuple(spec for _, _, spec in outs),
        scratch_shapes=scratch,
        cost_estimate=cost,
        compiler_params=pltpu.CompilerParams(vmem_limit_bytes=room * MIB),
    )(*args)


def share(value, axis):
    copies = jnp.broadcast_to(value[None], (lax.axis_size(axis),) + value.shape)
    return lax.all_to_all(copies, axis, 0, 0, tiled=True)


def by_pair(pairs, build, *args):
    branches = [functools.partial(build, pair) for pair in range(pairs)]
    if pairs == 1:
        return branches[0](*args)
    return lax.switch(lax.axis_index("layer") // FEAT_SPLIT, branches, *args)


def across(value, axis, step):
    pairs = [(i, i ^ step) for i in range(lax.axis_size(axis))]
    return lax.ppermute(value, axis, pairs)


def body(inputs, encoder, enc_bias, decoder, dec_bias, targets, top_index):
    tokens, layers, top_count = top_index.shape
    depth, width = encoder.shape[1:]
    feat = decoder.shape[3]
    slabs = lax.axis_size("lat")
    slab_most = 2 * top_count // slabs
    packed = tokens * layers * slab_most // LANES
    pairs = lax.axis_size("layer") // FEAT_SPLIT
    plan = (layers, width, top_count, slab_most)
    top = jnp.transpose(top_index, (1, 2, 0)).reshape(layers * top_count, tokens)
    dma = pltpu.SemaphoreType.DMA
    i16, i32 = jnp.int16, jnp.int32
    z, index, kept = call(
        functools.partial(encode_kernel, plan),
        [HBM] * 4,
        [
            ((packed, LANES), BF, VMEM),
            ((tokens, LANES), i16, VMEM),
            ((layers * slab_most, tokens), i32, VMEM),
        ],
        [
            pltpu.VMEM(inputs.shape, BF),
            pltpu.VMEM(encoder.shape, BF),
            pltpu.VMEM(enc_bias.shape, F32),
            pltpu.VMEM(top.shape, i32),
            pltpu.VMEM((layers, tokens, depth), BF),
            dma((4,)),
        ],
        inputs, encoder, enc_bias, top,
    )
    parts = share(z, "layer")
    (inverse,) = call(
        functools.partial(inverse_kernel, plan),
        [VMEM],
        [((layers, tokens, width), i16, VMEM)],
        [pltpu.VMEM((layers, 1 - (-width // (LANES * WORD_BLOCKS)), slab_most, tokens), i32)],
        kept,
        cost=pl.CostEstimate(flops=10**8, bytes_accessed=10**6, transcendentals=0),
    )

    def decode(pair, *args):
        return call(
            functools.partial(decode_kernel, plan, pair),
            [VMEM] * 4,
            [
                ((layers, tokens, width), BF, VMEM),
                ((tokens, feat), F32, VMEM),
                ((tokens, feat), F32, VMEM),
                ((tokens, feat), BF, VMEM),
                ((tokens, feat), BF, VMEM),
                ((tokens, LANES), i16, VMEM),
            ],
            [],
            *args,
        )

    act, mine_a, mine_b, sent_a, sent_b, index = by_pair(
        pairs, decode, parts, inverse, decoder[0], index
    )
    steps = [1 << i | 1 for i in range(slabs.bit_length() - 1)]
    for i in range(len(steps)):
        theirs_a = across(sent_a, "lat", steps[i])
        theirs_b = across(sent_b, "lat", steps[-1 - i])
        if i + 1 < len(steps):
            mine_a = mine_a + theirs_a.astype(F32)
            mine_b = mine_b + theirs_b.astype(F32)
            sent_a, sent_b = mine_a.astype(BF), mine_b.astype(BF)
            sent_a, act = lax.optimization_barrier((sent_a, act))
    act_t, x_t, targets_by_slot, decoder_t = call(
        turn_kernel,
        [VMEM] * 4,
        [
            ((layers, width, tokens), BF, VMEM),
            ((layers, depth, tokens), BF, VMEM),
            ((2, tokens, feat), BF, VMEM),
            ((layers + 1, feat, width), BF, VMEM),
        ],
        [],
        act, inputs, targets[0], decoder[0],
        cost=pl.CostEstimate(flops=10**8, bytes_accessed=10**7, transcendentals=0),
    )

    def residues(pair, *args):
        return call(
            functools.partial(residue_kernel, plan, pair),
            [VMEM] * 9,
            [
                ((packed, LANES), BF, VMEM),
                ((2, tokens, feat), BF, VMEM),
                ((width, feat), F32, VMEM),
            ],
            [],
            *args,
        )

    z, residue, head = by_pair(
        pairs, residues, mine_a, mine_b, theirs_a, theirs_b, dec_bias[0], targets_by_slot, index, decoder_t, act_t
    )
    parts = share(z, "layer")

    def grads(pair, *args):
        return call(
            functools.partial(grads_kernel, plan, pair),
            [VMEM] * 6,
            [
                ((layers + 1, width, feat), F32, HBM),
                (encoder.shape, F32, HBM),
                (enc_bias.shape, F32, HBM),
            ],
            [
                pltpu.VMEM((tokens, LANES), BF),
                pltpu.VMEM((layers, width, feat), F32),
                pltpu.VMEM(encoder.shape, F32),
                pltpu.VMEM(enc_bias.shape, F32),
                dma((PARTS * 2 * layers + 2,)),
            ],
            *args,
        )

    decoder_grad, encoder_grad, bias_grad = by_pair(
        pairs, grads, parts, inverse, x_t, act_t, residue, head
    )
    return decoder_grad[None], encoder_grad, bias_grad


def solution(mesh):
    return jax.shard_map(
        body,
        mesh=mesh,
        in_specs=(
            P(None, None, "layer"),
            P(None, "layer", "lat"),
            P(None, "lat"),
            P("layer", None, "lat", None),
            P("layer", None, None),
            P("layer", None, None, None),
            P(),
        ),
        out_specs=(P("layer", None, "lat", None), P(None, "layer", "lat"), P(None, "lat")),
        check_vma=False,
    )
```

```python
import functools

import jax
import jax.numpy as jnp
from jax import lax
from jax.experimental import pallas as pl
from jax.experimental.pallas import tpu as pltpu
from jax.sharding import PartitionSpec as P

FEAT_SPLIT = 8
LANES = 128
PARTS = 4
CHUNK = 32
NUMBER_BITS = 7
WORD_BLOCKS = 31 // NUMBER_BITS

BF = jnp.bfloat16
F32 = jnp.float32
NT = (((1,), (1,)), ((), ()))
TN = (((0,), (0,)), ((), ()))


def matmul(left, right, dims=(((1,), (0,)), ((), ()))):
    return lax.dot_general(left, right, dims, preferred_element_type=F32)


def flag(condition):
    return jnp.where(condition, 1.0, 0.0).astype(BF)


def iota(shape, dimension):
    return lax.broadcasted_iota(jnp.int32, shape, dimension)


def pick_lanes(table, lanes):
    return lax.gather(
        table,
        lanes[..., None],
        lax.GatherDimensionNumbers(
            offset_dims=(),
            collapsed_slice_dims=(1,),
            start_index_map=(1,),
            operand_batching_dims=(0,),
            start_indices_batching_dims=(0,),
        ),
        slice_sizes=(1, 1),
        mode=lax.GatherScatterMode.PROMISE_IN_BOUNDS,
    )


def choose(options, index, bit):
    while len(options) > 1:
        odd = jnp.bitwise_and(index, jnp.int16(bit)) != 0
        options = [
            jnp.where(odd, options[i + 1], options[i]) if i + 1 < len(options) else options[i]
            for i in range(0, len(options), 2)
        ]
        bit *= 2
    return options[0]


def stride(width):
    return 1 << (width // LANES - 1).bit_length()


def gather_slots(dense, index):
    lane = jnp.bitwise_and(index, jnp.int16(LANES - 1))
    picked = [
        pick_lanes(dense[:, b * LANES : (b + 1) * LANES].astype(BF), lane)
        for b in range(dense.shape[1] // LANES)
    ]
    return choose(picked, index, LANES)


def join_layers(picked, index, width):
    total = choose(picked, index, LANES * stride(width))
    return jnp.where(index < 0, jnp.zeros_like(total), total)


def fold_slots(values, used):
    rows = values.shape[0] * used // LANES
    total = values[:rows]
    for first in range(rows, values.shape[0], rows):
        total = total + values[first : first + rows]
    return total


def sum_parts(parts_ref, used):
    total = jnp.sum(parts_ref[...].astype(F32), axis=0)
    part = iota(total.shape, 1) // used
    return jnp.concatenate(
        [jnp.where(part == f, total, 0.0).astype(BF) for f in range(LANES // used)], axis=0
    )


def place_slots(values, lane):
    blocks = lane.shape[1] // LANES
    return jnp.concatenate(
        [pick_lanes(values, lane[:, b * LANES : (b + 1) * LANES]) for b in range(blocks)],
        axis=1,
    )


def slot_index(top, slab, width, layers, top_count, slab_most):
    rows, tokens = top.shape
    place = jnp.bitwise_and(iota(top.shape, 0), top_count - 1)
    local = top - slab * width
    inside = (local >= 0) & (local < width)
    after = iota((rows, rows), 0)
    before = iota((rows, rows), 1)
    earlier = flag((before // top_count == after // top_count) & (before < after))
    rank = matmul(earlier, flag(inside)).astype(jnp.int32)
    local = local + (iota(top.shape, 0) // top_count) * (stride(width) * LANES)
    word = jnp.where(inside, (1 << 30) + ((place - rank) << 16) + local, 0)
    step = 0
    while (1 << step) < top_count:
        moved = pltpu.roll(word, rows - (1 << step), 0)
        bit = 1 << (16 + step)
        word = jnp.where((moved & bit) != 0, moved, jnp.where((word & bit) != 0, 0, word))
        step += 1
    index = jnp.where(word != 0, word & 0xFFFF, -1)
    return jnp.concatenate(
        [index[layer * top_count : layer * top_count + slab_most] for layer in range(layers)], axis=0
    )


def by_token(kept):
    used, tokens = kept.shape
    folds = LANES // used
    part = iota(kept.shape, 1) // (tokens // folds)
    return jnp.transpose(
        jnp.concatenate([jnp.where(part == f, kept, -1) for f in range(folds)], axis=0), (1, 0)
    )


def inverse_kernel(plan, kept_ref, inverse_ref, rows_ref):
    layers, width, top_count, slab_most = plan
    tokens = kept_ref.shape[1]
    blocks = width // LANES
    words = -(-blocks // WORD_BLOCKS)
    used = layers * slab_most
    part = iota((tokens, LANES), 0) // (tokens * used // LANES)
    unused = (part + 1) % (LANES // used) * used
    for layer in range(layers):
        own = kept_ref[layer * slab_most : (layer + 1) * slab_most, :]
        block = lax.shift_right_arithmetic(own, 7) - layer * stride(width)
        number = iota(own.shape, 0) + (1 + layer * slab_most)
        value = lax.shift_left(number, NUMBER_BITS * (block % WORD_BLOCKS))
        rows_ref[layer, 0] = jnp.bitwise_and(own, LANES - 1)
        for w in range(words):
            rows_ref[layer, 1 + w] = jnp.where((own >= 0) & (block // WORD_BLOCKS == w), value, 0)
        pieces = [[] for w in range(words)]
        for first in range(0, LANES, CHUNK):
            lane = iota((CHUNK, tokens), 0) + first
            totals = [jnp.zeros((CHUNK, tokens), jnp.int32) for w in range(words)]
            for s in range(slab_most):
                match = lane == rows_ref[layer, 0, s : s + 1, :]
                for w in range(words):
                    totals[w] = totals[w] + jnp.where(match, rows_ref[layer, 1 + w, s : s + 1, :], 0)
            for w in range(words):
                pieces[w].append(totals[w])
        for w in range(words):
            word = jnp.transpose(jnp.concatenate(pieces[w], axis=0), (1, 0))
            for b in range(w * WORD_BLOCKS, min((w + 1) * WORD_BLOCKS, blocks)):
                numbers = lax.shift_right_logical(word, NUMBER_BITS * (b % WORD_BLOCKS))
                numbers = jnp.bitwise_and(numbers, LANES - 1)
                lanes = jnp.where(numbers > 0, numbers - 1 + part * used, unused)
                inverse_ref[layer, :, b * LANES : (b + 1) * LANES] = lanes.astype(jnp.int16)


def encode_kernel(
    plan, x_hbm, encoder_hbm, bias_hbm, top_hbm, z_ref, index_ref, kept_ref,
    x_ref, encoder_ref, bias_ref, top_ref, x_layer, sems
):
    layers, width, top_count, slab_most = plan
    copies = [
        pltpu.make_async_copy(source, target, sems.at[i])
        for i, (source, target) in enumerate(
            [(top_hbm, top_ref), (x_hbm, x_ref), (bias_hbm, bias_ref), (encoder_hbm, encoder_ref)]
        )
    ]
    for copy in copies:
        copy.start()
    for copy in copies[:2]:
        copy.wait()
    tokens, depth = x_ref.shape[0], x_ref.shape[2]
    x_rows = x_ref[...].reshape(tokens * layers, depth)
    token, row = iota((tokens, tokens * layers), 0), iota((tokens, tokens * layers), 1)
    for layer in range(layers):
        x_layer[layer] = matmul(flag(row == layers * token + layer), x_rows).astype(BF)
    kept = slot_index(top_ref[...], lax.axis_index("lat"), width, layers, top_count, slab_most)
    kept_ref[...] = kept
    index = by_token(kept).astype(jnp.int16)
    index_ref[...] = index
    for copy in copies[2:]:
        copy.wait()
    with_bias = jnp.where(lax.axis_index("layer") == 0, 1.0, 0.0)
    picked = []
    for layer in range(layers):
        dense = matmul(x_layer[layer], encoder_ref[layer])
        dense = dense + bias_ref[layer : layer + 1, :] * with_bias
        picked.append(gather_slots(dense, index))
    z_ref[...] = fold_slots(join_layers(picked, index, width), layers * slab_most)


def block_places(layers, pair):
    return [(k, 0) if k <= pair else (k - pair - 1, 1) for k in range(layers + 1)]


def decode_kernel(
    plan, pair, parts_ref, inverse_ref, decoder_ref, index_ref,
    act_ref, first_ref, second_ref, first_rounded, second_rounded, index_out
):
    layers, width, top_count, slab_most = plan
    index_out[...] = index_ref[...]
    total = sum_parts(parts_ref, layers * slab_most)
    for layer in range(layers):
        act_ref[layer] = place_slots(total, inverse_ref[layer])
    sums = [None, None]
    for k, (source, slot) in enumerate(block_places(layers, pair)):
        term = matmul(act_ref[source], decoder_ref[k])
        sums[slot] = term if sums[slot] is None else sums[slot] + term
    first_ref[...] = sums[0]
    second_ref[...] = sums[1]
    first_rounded[...] = sums[0].astype(BF)
    second_rounded[...] = sums[1].astype(BF)


def turn_kernel(act_ref, x_ref, targets_ref, decoder_ref, act_t, x_t, targets_out, decoder_t):
    for layer in range(act_ref.shape[0]):
        act_t[layer] = jnp.transpose(act_ref[layer], (1, 0))
        x_t[layer] = jnp.transpose(x_ref[:, layer, :], (1, 0))
    for slot in range(2):
        targets_out[slot] = targets_ref[:, slot, :]
    for k in range(decoder_ref.shape[0]):
        decoder_t[k] = jnp.transpose(decoder_ref[k], (1, 0))


def residue_kernel(
    plan, pair, mine_a, mine_b, theirs_a, theirs_b, dec_bias_ref, targets_ref, index_ref, decoder_t,
    act_t, z_ref, residue, head_ref
):
    layers, width, top_count, slab_most = plan
    for slot, (mine, theirs) in enumerate([(mine_a, theirs_a), (mine_b, theirs_b)]):
        rebuilt = mine[...] + theirs[...].astype(F32)
        rebuilt = rebuilt + dec_bias_ref[slot : slot + 1, :]
        residue[slot] = (rebuilt - targets_ref[slot].astype(F32)).astype(BF)
    places = block_places(layers, pair)
    index = index_ref[...]
    picked = []
    for layer in range(layers):
        dense = None
        for k, (source, slot) in enumerate(places):
            if source == layer:
                term = matmul(residue[slot], decoder_t[k])
                dense = term if dense is None else dense + term
        picked.append(jnp.zeros(index.shape, BF) if dense is None else gather_slots(dense, index))
    z_ref[...] = fold_slots(join_layers(picked, index, width), layers * slab_most)
    head_ref[...] = matmul(act_t[places[0][0]], residue[places[0][1]])


def grads_kernel(
    plan, pair, parts_ref, inverse_ref, x_t, act_t, residue_ref, head_ref,
    decoder_hbm, encoder_hbm, bias_hbm, values, decoder_grad, encoder_grad, bias, sems
):
    layers, width, top_count, slab_most = plan
    tokens = x_t.shape[2]
    part = width // PARTS
    copies = []

    def send(source, target):
        copies.append(pltpu.make_async_copy(source, target, sems.at[len(copies)]))
        copies[-1].start()

    send(head_ref, decoder_hbm.at[0])
    values[...] = sum_parts(parts_ref, layers * slab_most)
    ones = jnp.ones((8, tokens), BF)
    for layer in range(layers):
        for i in range(PARTS):
            at = (layer, slice(None), pl.ds(i * part, part))
            dense = place_slots(values[...], inverse_ref[at])
            encoder_grad[at] = matmul(x_t[layer], dense)
            send(encoder_grad.at[at], encoder_hbm.at[at])
            bias[layer : layer + 1, i * part : (i + 1) * part] = matmul(ones, dense)[:1]
    for k, (source, slot) in list(enumerate(block_places(layers, pair)))[1:]:
        for i in range(PARTS):
            rows = pl.ds(i * part, part)
            decoder_grad[k - 1, rows] = matmul(act_t[source, rows], residue_ref[slot])
            send(decoder_grad.at[k - 1, rows], decoder_hbm.at[k, rows])
    send(bias, bias_hbm)
    for copy in copies:
        copy.wait()


VMEM = pl.BlockSpec(memory_space=pltpu.VMEM)
HBM = pl.BlockSpec(memory_space=pltpu.HBM)
MIB = 1024 * 1024


def call(kernel, ins, outs, scratch, *args, cost=None, room=24):
    args = [
        pltpu.with_memory_space_constraint(arg, pltpu.HBM) if spec is HBM else arg
        for spec, arg in zip(ins, args, strict=True)
    ]
    return pl.pallas_call(
        kernel,
        out_shape=tuple(
            (pltpu.HBM if spec is HBM else pltpu.VMEM)(shape, dtype) for shape, dtype, spec in outs
        ),
        in_specs=ins,
        out_specs=tuple(spec for _, _, spec in outs),
        scratch_shapes=scratch,
        cost_estimate=cost,
        compiler_params=pltpu.CompilerParams(vmem_limit_bytes=room * MIB),
    )(*args)


def share(value, axis):
    copies = jnp.broadcast_to(value[None], (lax.axis_size(axis),) + value.shape)
    return lax.all_to_all(copies, axis, 0, 0, tiled=True)


def by_pair(pairs, build, *args):
    branches = [functools.partial(build, pair) for pair in range(pairs)]
    if pairs == 1:
        return branches[0](*args)
    return lax.switch(lax.axis_index("layer") // FEAT_SPLIT, branches, *args)


def across(value, axis, step):
    pairs = [(i, i ^ step) for i in range(lax.axis_size(axis))]
    return lax.ppermute(value, axis, pairs)


def body(inputs, encoder, enc_bias, decoder, dec_bias, targets, top_index):
    tokens, layers, top_count = top_index.shape
    depth, width = encoder.shape[1:]
    feat = decoder.shape[3]
    slabs = lax.axis_size("lat")
    slab_most = 2 * top_count // slabs
    packed = tokens * layers * slab_most // LANES
    pairs = lax.axis_size("layer") // FEAT_SPLIT
    plan = (layers, width, top_count, slab_most)
    top = jnp.transpose(top_index, (1, 2, 0)).reshape(layers * top_count, tokens)
    dma = pltpu.SemaphoreType.DMA
    i16, i32 = jnp.int16, jnp.int32
    z, index, kept = call(
        functools.partial(encode_kernel, plan),
        [HBM] * 4,
        [
            ((packed, LANES), BF, VMEM),
            ((tokens, LANES), i16, VMEM),
            ((layers * slab_most, tokens), i32, VMEM),
        ],
        [
            pltpu.VMEM(inputs.shape, BF),
            pltpu.VMEM(encoder.shape, BF),
            pltpu.VMEM(enc_bias.shape, F32),
            pltpu.VMEM(top.shape, i32),
            pltpu.VMEM((layers, tokens, depth), BF),
            dma((4,)),
        ],
        inputs, encoder, enc_bias, top,
    )
    parts = share(z, "layer")
    (inverse,) = call(
        functools.partial(inverse_kernel, plan),
        [VMEM],
        [((layers, tokens, width), i16, VMEM)],
        [pltpu.VMEM((layers, 1 - (-width // (LANES * WORD_BLOCKS)), slab_most, tokens), i32)],
        kept,
        cost=pl.CostEstimate(flops=10**8, bytes_accessed=10**6, transcendentals=0),
    )

    def decode(pair, *args):
        return call(
            functools.partial(decode_kernel, plan, pair),
            [VMEM] * 4,
            [
                ((layers, tokens, width), BF, VMEM),
                ((tokens, feat), F32, VMEM),
                ((tokens, feat), F32, VMEM),
                ((tokens, feat), BF, VMEM),
                ((tokens, feat), BF, VMEM),
                ((tokens, LANES), i16, VMEM),
            ],
            [],
            *args,
        )

    act, mine_a, mine_b, sent_a, sent_b, index = by_pair(
        pairs, decode, parts, inverse, decoder[0], index
    )
    def turn(act):
        return call(
            turn_kernel,
            [VMEM] * 4,
            [
                ((layers, width, tokens), BF, VMEM),
                ((layers, depth, tokens), BF, VMEM),
                ((2, tokens, feat), BF, VMEM),
                ((layers + 1, feat, width), BF, VMEM),
            ],
            [],
            act, inputs, targets[0], decoder[0],
            cost=pl.CostEstimate(flops=10**8, bytes_accessed=10**7, transcendentals=0),
        )

    steps = [1 << i | 1 for i in range(slabs.bit_length() - 1)]
    turned = None
    for i in range(len(steps)):
        theirs_a = across(sent_a, "lat", 1 << i)
        theirs_b = across(sent_b, "lat", steps[-1 - i])
        if i + 1 < len(steps):
            mine_a = mine_a + theirs_a.astype(F32)
            sent_a = mine_a.astype(BF)
            if i + 2 == len(steps):
                sent_a, act = lax.optimization_barrier((sent_a, act))
                turned = turn(act)
            mine_b = mine_b + theirs_b.astype(F32)
            sent_b = mine_b.astype(BF)
            if turned is not None:
                sent_b, turned = lax.optimization_barrier((sent_b, turned))
    act_t, x_t, targets_by_slot, decoder_t = turn(act) if turned is None else turned

    def residues(pair, *args):
        return call(
            functools.partial(residue_kernel, plan, pair),
            [VMEM] * 9,
            [
                ((packed, LANES), BF, VMEM),
                ((2, tokens, feat), BF, VMEM),
                ((width, feat), F32, VMEM),
            ],
            [],
            *args,
        )

    z, residue, head = by_pair(
        pairs, residues, mine_a, mine_b, theirs_a, theirs_b, dec_bias[0], targets_by_slot, index, decoder_t, act_t
    )
    parts = share(z, "layer")

    def grads(pair, *args):
        return call(
            functools.partial(grads_kernel, plan, pair),
            [VMEM] * 6,
            [
                ((layers + 1, width, feat), F32, HBM),
                (encoder.shape, F32, HBM),
                (enc_bias.shape, F32, HBM),
            ],
            [
                pltpu.VMEM((tokens, LANES), BF),
                pltpu.VMEM((layers, width, feat), F32),
                pltpu.VMEM(encoder.shape, F32),
                pltpu.VMEM(enc_bias.shape, F32),
                dma((PARTS * 2 * layers + 2,)),
            ],
            *args,
        )

    decoder_grad, encoder_grad, bias_grad = by_pair(
        pairs, grads, parts, inverse, x_t, act_t, residue, head
    )
    return decoder_grad[None], encoder_grad, bias_grad


def solution(mesh):
    return jax.shard_map(
        body,
        mesh=mesh,
        in_specs=(
            P(None, None, "layer"),
            P(None, "layer", "lat"),
            P(None, "lat"),
            P("layer", None, "lat", None),
            P("layer", None, None),
            P("layer", None, None, None),
            P(),
        ),
        out_specs=(P("layer", None, "lat", None), P(None, "layer", "lat"), P(None, "lat")),
        check_vma=False,
    )
```

```python
import functools

import jax
import jax.numpy as jnp
from jax import lax
from jax.experimental import pallas as pl
from jax.experimental.pallas import tpu as pltpu
from jax.sharding import PartitionSpec as P

FEAT_SPLIT = 8
LANES = 128
PARTS = 4
CHUNK = 32
NUMBER_BITS = 7
WORD_BLOCKS = 31 // NUMBER_BITS

BF = jnp.bfloat16
F32 = jnp.float32
NT = (((1,), (1,)), ((), ()))
TN = (((0,), (0,)), ((), ()))


def matmul(left, right, dims=(((1,), (0,)), ((), ()))):
    return lax.dot_general(left, right, dims, preferred_element_type=F32)


def flag(condition):
    return jnp.where(condition, 1.0, 0.0).astype(BF)


def iota(shape, dimension):
    return lax.broadcasted_iota(jnp.int32, shape, dimension)


def pick_lanes(table, lanes):
    return lax.gather(
        table,
        lanes[..., None],
        lax.GatherDimensionNumbers(
            offset_dims=(),
            collapsed_slice_dims=(1,),
            start_index_map=(1,),
            operand_batching_dims=(0,),
            start_indices_batching_dims=(0,),
        ),
        slice_sizes=(1, 1),
        mode=lax.GatherScatterMode.PROMISE_IN_BOUNDS,
    )


def choose(options, index, bit):
    while len(options) > 1:
        odd = jnp.bitwise_and(index, jnp.int16(bit)) != 0
        options = [
            jnp.where(odd, options[i + 1], options[i]) if i + 1 < len(options) else options[i]
            for i in range(0, len(options), 2)
        ]
        bit *= 2
    return options[0]


def stride(width):
    return 1 << (width // LANES - 1).bit_length()


def gather_slots(dense, index):
    lane = jnp.bitwise_and(index, jnp.int16(LANES - 1))
    picked = [
        pick_lanes(dense[:, b * LANES : (b + 1) * LANES].astype(BF), lane)
        for b in range(dense.shape[1] // LANES)
    ]
    return choose(picked, index, LANES)


def join_layers(picked, index, width):
    total = choose(picked, index, LANES * stride(width))
    return jnp.where(index < 0, jnp.zeros_like(total), total)


def fold_slots(values, used):
    rows = values.shape[0] * used // LANES
    total = values[:rows]
    for first in range(rows, values.shape[0], rows):
        total = total + values[first : first + rows]
    return total


def sum_parts(parts_ref, used):
    total = jnp.sum(parts_ref[...].astype(F32), axis=0)
    part = iota(total.shape, 1) // used
    return jnp.concatenate(
        [jnp.where(part == f, total, 0.0).astype(BF) for f in range(LANES // used)], axis=0
    )


def place_slots(values, lane):
    blocks = lane.shape[1] // LANES
    return jnp.concatenate(
        [pick_lanes(values, lane[:, b * LANES : (b + 1) * LANES]) for b in range(blocks)],
        axis=1,
    )


def slot_index(top, slab, width, layers, top_count, slab_most):
    rows, tokens = top.shape
    place = jnp.bitwise_and(iota(top.shape, 0), top_count - 1)
    local = top - slab * width
    inside = (local >= 0) & (local < width)
    after = iota((rows, rows), 0)
    before = iota((rows, rows), 1)
    earlier = flag((before // top_count == after // top_count) & (before < after))
    rank = matmul(earlier, flag(inside)).astype(jnp.int32)
    local = local + (iota(top.shape, 0) // top_count) * (stride(width) * LANES)
    word = jnp.where(inside, (1 << 30) + ((place - rank) << 16) + local, 0)
    step = 0
    while (1 << step) < top_count:
        moved = pltpu.roll(word, rows - (1 << step), 0)
        bit = 1 << (16 + step)
        word = jnp.where((moved & bit) != 0, moved, jnp.where((word & bit) != 0, 0, word))
        step += 1
    index = jnp.where(word != 0, word & 0xFFFF, -1)
    return jnp.concatenate(
        [index[layer * top_count : layer * top_count + slab_most] for layer in range(layers)], axis=0
    )


def by_token(kept):
    used, tokens = kept.shape
    folds = LANES // used
    part = iota(kept.shape, 1) // (tokens // folds)
    return jnp.transpose(
        jnp.concatenate([jnp.where(part == f, kept, -1) for f in range(folds)], axis=0), (1, 0)
    )


def inverse_kernel(plan, kept_ref, inverse_ref, rows_ref):
    layers, width, top_count, slab_most = plan
    tokens = kept_ref.shape[1]
    blocks = width // LANES
    words = -(-blocks // WORD_BLOCKS)
    used = layers * slab_most
    part = iota((tokens, LANES), 0) // (tokens * used // LANES)
    unused = (part + 1) % (LANES // used) * used
    for layer in range(layers):
        own = kept_ref[layer * slab_most : (layer + 1) * slab_most, :]
        block = lax.shift_right_arithmetic(own, 7) - layer * stride(width)
        number = iota(own.shape, 0) + (1 + layer * slab_most)
        value = lax.shift_left(number, NUMBER_BITS * (block % WORD_BLOCKS))
        rows_ref[layer, 0] = jnp.bitwise_and(own, LANES - 1)
        for w in range(words):
            rows_ref[layer, 1 + w] = jnp.where((own >= 0) & (block // WORD_BLOCKS == w), value, 0)
        pieces = [[] for w in range(words)]
        for first in range(0, LANES, CHUNK):
            lane = iota((CHUNK, tokens), 0) + first
            totals = [jnp.zeros((CHUNK, tokens), jnp.int32) for w in range(words)]
            for s in range(slab_most):
                match = lane == rows_ref[layer, 0, s : s + 1, :]
                for w in range(words):
                    totals[w] = totals[w] + jnp.where(match, rows_ref[layer, 1 + w, s : s + 1, :], 0)
            for w in range(words):
                pieces[w].append(totals[w])
        for w in range(words):
            word = jnp.transpose(jnp.concatenate(pieces[w], axis=0), (1, 0))
            for b in range(w * WORD_BLOCKS, min((w + 1) * WORD_BLOCKS, blocks)):
                numbers = lax.shift_right_logical(word, NUMBER_BITS * (b % WORD_BLOCKS))
                numbers = jnp.bitwise_and(numbers, LANES - 1)
                lanes = jnp.where(numbers > 0, numbers - 1 + part * used, unused)
                inverse_ref[layer, :, b * LANES : (b + 1) * LANES] = lanes.astype(jnp.int16)


def encode_kernel(
    plan, x_hbm, encoder_hbm, bias_hbm, top_hbm, z_ref, index_ref, kept_ref,
    x_ref, encoder_ref, bias_ref, top_ref, x_layer, sems
):
    layers, width, top_count, slab_most = plan
    copies = [
        pltpu.make_async_copy(source, target, sems.at[i])
        for i, (source, target) in enumerate(
            [(top_hbm, top_ref), (x_hbm, x_ref), (bias_hbm, bias_ref), (encoder_hbm, encoder_ref)]
        )
    ]
    for copy in copies:
        copy.start()
    for copy in copies[:2]:
        copy.wait()
    tokens, depth = x_ref.shape[0], x_ref.shape[2]
    x_rows = x_ref[...].reshape(tokens * layers, depth)
    token, row = iota((tokens, tokens * layers), 0), iota((tokens, tokens * layers), 1)
    for layer in range(layers):
        x_layer[layer] = matmul(flag(row == layers * token + layer), x_rows).astype(BF)
    kept = slot_index(top_ref[...], lax.axis_index("lat"), width, layers, top_count, slab_most)
    kept_ref[...] = kept
    index = by_token(kept).astype(jnp.int16)
    index_ref[...] = index
    for copy in copies[2:]:
        copy.wait()
    with_bias = jnp.where(lax.axis_index("layer") == 0, 1.0, 0.0)
    picked = []
    for layer in range(layers):
        dense = matmul(x_layer[layer], encoder_ref[layer])
        dense = dense + bias_ref[layer : layer + 1, :] * with_bias
        picked.append(gather_slots(dense, index))
    z_ref[...] = fold_slots(join_layers(picked, index, width), layers * slab_most)


def block_places(layers, pair):
    return [(k, 0) if k <= pair else (k - pair - 1, 1) for k in range(layers + 1)]


def decode_kernel(
    plan, pair, parts_ref, inverse_ref, decoder_ref, index_ref,
    act_ref, first_ref, second_ref, first_rounded, second_rounded, index_out
):
    layers, width, top_count, slab_most = plan
    index_out[...] = index_ref[...]
    total = sum_parts(parts_ref, layers * slab_most)
    sums = [None, None]
    places = block_places(layers, pair)
    for layer in range(layers):
        for first in range(0, width, 2 * LANES):
            columns = slice(first, first + 2 * LANES)
            piece = place_slots(total, inverse_ref[layer, :, columns])
            act_ref[layer, :, columns] = piece
            for k, (source, slot) in enumerate(places):
                if source == layer:
                    term = matmul(piece, decoder_ref[k, columns, :])
                    sums[slot] = term if sums[slot] is None else sums[slot] + term
    first_ref[...] = sums[0]
    second_ref[...] = sums[1]
    first_rounded[...] = sums[0].astype(BF)
    second_rounded[...] = sums[1].astype(BF)


def turn_kernel(act_ref, x_ref, targets_ref, decoder_ref, act_t, x_t, targets_out, decoder_t):
    for layer in range(act_ref.shape[0]):
        act_t[layer] = jnp.transpose(act_ref[layer], (1, 0))
        x_t[layer] = jnp.transpose(x_ref[:, layer, :], (1, 0))
    for slot in range(2):
        targets_out[slot] = targets_ref[:, slot, :]
    for k in range(decoder_ref.shape[0]):
        decoder_t[k] = jnp.transpose(decoder_ref[k], (1, 0))


def residue_kernel(
    plan, pair, mine_a, mine_b, theirs_a, theirs_b, dec_bias_ref, targets_ref, index_ref, decoder_t,
    act_t, z_ref, residue, head_ref
):
    layers, width, top_count, slab_most = plan
    for slot, (mine, theirs) in enumerate([(mine_a, theirs_a), (mine_b, theirs_b)]):
        rebuilt = mine[...] + theirs[...].astype(F32)
        rebuilt = rebuilt + dec_bias_ref[slot : slot + 1, :]
        residue[slot] = (rebuilt - targets_ref[slot].astype(F32)).astype(BF)
    places = block_places(layers, pair)
    index = index_ref[...]
    picked = []
    for layer in range(layers):
        own = [(k, slot) for k, (source, slot) in enumerate(places) if source == layer]
        if own:
            left = jnp.concatenate([residue[slot] for k, slot in own], axis=1)
            right = jnp.concatenate([decoder_t[k] for k, slot in own], axis=0)
            picked.append(gather_slots(matmul(left, right), index))
        else:
            picked.append(jnp.zeros(index.shape, BF))
    z_ref[...] = fold_slots(join_layers(picked, index, width), layers * slab_most)
    head_ref[...] = matmul(act_t[places[0][0]], residue[places[0][1]])


def grads_kernel(
    plan, pair, parts_ref, inverse_ref, x_t, act_t, residue_ref, head_ref,
    decoder_hbm, encoder_hbm, bias_hbm, values, decoder_grad, encoder_grad, bias, sems
):
    layers, width, top_count, slab_most = plan
    tokens = x_t.shape[2]
    part = width // PARTS
    copies = []

    def send(source, target):
        copies.append(pltpu.make_async_copy(source, target, sems.at[len(copies)]))
        copies[-1].start()

    send(head_ref, decoder_hbm.at[0])
    values[...] = sum_parts(parts_ref, layers * slab_most)
    ones = jnp.ones((8, tokens), BF)
    for layer in range(layers):
        for i in range(PARTS):
            at = (layer, slice(None), pl.ds(i * part, part))
            dense = place_slots(values[...], inverse_ref[at])
            encoder_grad[at] = matmul(x_t[layer], dense)
            send(encoder_grad.at[at], encoder_hbm.at[at])
            bias[layer : layer + 1, i * part : (i + 1) * part] = matmul(ones, dense)[:1]
    for k, (source, slot) in list(enumerate(block_places(layers, pair)))[1:]:
        for i in range(PARTS):
            rows = pl.ds(i * part, part)
            decoder_grad[k - 1, rows] = matmul(act_t[source, rows], residue_ref[slot])
            send(decoder_grad.at[k - 1, rows], decoder_hbm.at[k, rows])
    send(bias, bias_hbm)
    for copy in copies:
        copy.wait()


VMEM = pl.BlockSpec(memory_space=pltpu.VMEM)
HBM = pl.BlockSpec(memory_space=pltpu.HBM)
MIB = 1024 * 1024


def call(kernel, ins, outs, scratch, *args, cost=None, room=24):
    args = [
        pltpu.with_memory_space_constraint(arg, pltpu.HBM) if spec is HBM else arg
        for spec, arg in zip(ins, args, strict=True)
    ]
    return pl.pallas_call(
        kernel,
        out_shape=tuple(
            (pltpu.HBM if spec is HBM else pltpu.VMEM)(shape, dtype) for shape, dtype, spec in outs
        ),
        in_specs=ins,
        out_specs=tuple(spec for _, _, spec in outs),
        scratch_shapes=scratch,
        cost_estimate=cost,
        compiler_params=pltpu.CompilerParams(vmem_limit_bytes=room * MIB),
    )(*args)


def share(value, axis):
    copies = jnp.broadcast_to(value[None], (lax.axis_size(axis),) + value.shape)
    return lax.all_to_all(copies, axis, 0, 0, tiled=True)


def by_pair(pairs, build, *args):
    branches = [functools.partial(build, pair) for pair in range(pairs)]
    if pairs == 1:
        return branches[0](*args)
    return lax.switch(lax.axis_index("layer") // FEAT_SPLIT, branches, *args)


def across(value, axis, step):
    pairs = [(i, i ^ step) for i in range(lax.axis_size(axis))]
    return lax.ppermute(value, axis, pairs)


def body(inputs, encoder, enc_bias, decoder, dec_bias, targets, top_index):
    tokens, layers, top_count = top_index.shape
    depth, width = encoder.shape[1:]
    feat = decoder.shape[3]
    slabs = lax.axis_size("lat")
    slab_most = 2 * top_count // slabs
    packed = tokens * layers * slab_most // LANES
    pairs = lax.axis_size("layer") // FEAT_SPLIT
    plan = (layers, width, top_count, slab_most)
    top = jnp.transpose(top_index, (1, 2, 0)).reshape(layers * top_count, tokens)
    dma = pltpu.SemaphoreType.DMA
    i16, i32 = jnp.int16, jnp.int32
    z, index, kept = call(
        functools.partial(encode_kernel, plan),
        [HBM] * 4,
        [
            ((packed, LANES), BF, VMEM),
            ((tokens, LANES), i16, VMEM),
            ((layers * slab_most, tokens), i32, VMEM),
        ],
        [
            pltpu.VMEM(inputs.shape, BF),
            pltpu.VMEM(encoder.shape, BF),
            pltpu.VMEM(enc_bias.shape, F32),
            pltpu.VMEM(top.shape, i32),
            pltpu.VMEM((layers, tokens, depth), BF),
            dma((4,)),
        ],
        inputs, encoder, enc_bias, top,
    )
    parts = share(z, "layer")
    (inverse,) = call(
        functools.partial(inverse_kernel, plan),
        [VMEM],
        [((layers, tokens, width), i16, VMEM)],
        [pltpu.VMEM((layers, 1 - (-width // (LANES * WORD_BLOCKS)), slab_most, tokens), i32)],
        kept,
        cost=pl.CostEstimate(flops=10**8, bytes_accessed=10**6, transcendentals=0),
    )

    def decode(pair, *args):
        return call(
            functools.partial(decode_kernel, plan, pair),
            [VMEM] * 4,
            [
                ((layers, tokens, width), BF, VMEM),
                ((tokens, feat), F32, VMEM),
                ((tokens, feat), F32, VMEM),
                ((tokens, feat), BF, VMEM),
                ((tokens, feat), BF, VMEM),
                ((tokens, LANES), i16, VMEM),
            ],
            [],
            *args,
        )

    act, mine_a, mine_b, sent_a, sent_b, index = by_pair(
        pairs, decode, parts, inverse, decoder[0], index
    )
    def turn(act):
        return call(
            turn_kernel,
            [VMEM] * 4,
            [
                ((layers, width, tokens), BF, VMEM),
                ((layers, depth, tokens), BF, VMEM),
                ((2, tokens, feat), BF, VMEM),
                ((layers + 1, feat, width), BF, VMEM),
            ],
            [],
            act, inputs, targets[0], decoder[0],
            cost=pl.CostEstimate(flops=10**8, bytes_accessed=10**7, transcendentals=0),
        )

    steps = [1 << i | 1 for i in range(slabs.bit_length() - 1)]
    turned = None
    for i in range(len(steps)):
        theirs_a = across(sent_a, "lat", 1 << i)
        theirs_b = across(sent_b, "lat", steps[-1 - i])
        if i + 1 < len(steps):
            mine_a = mine_a + theirs_a.astype(F32)
            sent_a = mine_a.astype(BF)
            if i + 2 == len(steps):
                sent_a, act = lax.optimization_barrier((sent_a, act))
                turned = turn(act)
            mine_b = mine_b + theirs_b.astype(F32)
            sent_b = mine_b.astype(BF)
            if turned is not None:
                sent_b, turned = lax.optimization_barrier((sent_b, turned))
    act_t, x_t, targets_by_slot, decoder_t = turn(act) if turned is None else turned

    def residues(pair, *args):
        return call(
            functools.partial(residue_kernel, plan, pair),
            [VMEM] * 9,
            [
                ((packed, LANES), BF, VMEM),
                ((2, tokens, feat), BF, VMEM),
                ((width, feat), F32, VMEM),
            ],
            [],
            *args,
        )

    z, residue, head = by_pair(
        pairs, residues, mine_a, mine_b, theirs_a, theirs_b, dec_bias[0], targets_by_slot, index, decoder_t, act_t
    )
    parts = share(z, "layer")

    def grads(pair, *args):
        return call(
            functools.partial(grads_kernel, plan, pair),
            [VMEM] * 6,
            [
                ((layers + 1, width, feat), F32, HBM),
                (encoder.shape, F32, HBM),
                (enc_bias.shape, F32, HBM),
            ],
            [
                pltpu.VMEM((tokens, LANES), BF),
                pltpu.VMEM((layers, width, feat), F32),
                pltpu.VMEM(encoder.shape, F32),
                pltpu.VMEM(enc_bias.shape, F32),
                dma((PARTS * 2 * layers + 2,)),
            ],
            *args,
        )

    decoder_grad, encoder_grad, bias_grad = by_pair(
        pairs, grads, parts, inverse, x_t, act_t, residue, head
    )
    return decoder_grad[None], encoder_grad, bias_grad


def solution(mesh):
    return jax.shard_map(
        body,
        mesh=mesh,
        in_specs=(
            P(None, None, "layer"),
            P(None, "layer", "lat"),
            P(None, "lat"),
            P("layer", None, "lat", None),
            P("layer", None, None),
            P("layer", None, None, None),
            P(),
        ),
        out_specs=(P("layer", None, "lat", None), P(None, "layer", "lat"), P(None, "lat")),
        check_vma=False,
    )
```

```python
import functools

import jax
import jax.numpy as jnp
from jax import lax
from jax.experimental import pallas as pl
from jax.experimental.pallas import tpu as pltpu
from jax.sharding import PartitionSpec as P

FEAT_SPLIT = 8
LANES = 128
PARTS = 4
CHUNK = 32
NUMBER_BITS = 7
WORD_BLOCKS = 31 // NUMBER_BITS

BF = jnp.bfloat16
F32 = jnp.float32
NT = (((1,), (1,)), ((), ()))
TN = (((0,), (0,)), ((), ()))


def matmul(left, right, dims=(((1,), (0,)), ((), ()))):
    return lax.dot_general(left, right, dims, preferred_element_type=F32)


def flag(condition):
    return jnp.where(condition, 1.0, 0.0).astype(BF)


def iota(shape, dimension):
    return lax.broadcasted_iota(jnp.int32, shape, dimension)


def pick_lanes(table, lanes):
    return lax.gather(
        table,
        lanes[..., None],
        lax.GatherDimensionNumbers(
            offset_dims=(),
            collapsed_slice_dims=(1,),
            start_index_map=(1,),
            operand_batching_dims=(0,),
            start_indices_batching_dims=(0,),
        ),
        slice_sizes=(1, 1),
        mode=lax.GatherScatterMode.PROMISE_IN_BOUNDS,
    )


def choose(options, index, bit):
    while len(options) > 1:
        odd = jnp.bitwise_and(index, jnp.int16(bit)) != 0
        options = [
            jnp.where(odd, options[i + 1], options[i]) if i + 1 < len(options) else options[i]
            for i in range(0, len(options), 2)
        ]
        bit *= 2
    return options[0]


def stride(width):
    return 1 << (width // LANES - 1).bit_length()


def gather_slots(dense, index):
    lane = jnp.bitwise_and(index, jnp.int16(LANES - 1))
    picked = [
        pick_lanes(dense[:, b * LANES : (b + 1) * LANES].astype(BF), lane)
        for b in range(dense.shape[1] // LANES)
    ]
    return choose(picked, index, LANES)


def join_layers(picked, index, width):
    total = choose(picked, index, LANES * stride(width))
    return jnp.where(index < 0, jnp.zeros_like(total), total)


def fold_slots(values, used):
    rows = values.shape[0] * used // LANES
    total = values[:rows]
    for first in range(rows, values.shape[0], rows):
        total = total + values[first : first + rows]
    return total


def sum_parts(parts_ref, used):
    total = jnp.sum(parts_ref[...].astype(F32), axis=0)
    part = iota(total.shape, 1) // used
    return jnp.concatenate(
        [jnp.where(part == f, total, 0.0).astype(BF) for f in range(LANES // used)], axis=0
    )


def place_slots(values, lane):
    blocks = lane.shape[1] // LANES
    return jnp.concatenate(
        [pick_lanes(values, lane[:, b * LANES : (b + 1) * LANES]) for b in range(blocks)],
        axis=1,
    )


def slot_index(top, slab, width, layers, top_count, slab_most):
    rows, tokens = top.shape
    place = jnp.bitwise_and(iota(top.shape, 0), top_count - 1)
    local = top - slab * width
    inside = (local >= 0) & (local < width)
    after = iota((rows, rows), 0)
    before = iota((rows, rows), 1)
    earlier = flag((before // top_count == after // top_count) & (before < after))
    rank = matmul(earlier, flag(inside)).astype(jnp.int32)
    local = local + (iota(top.shape, 0) // top_count) * (stride(width) * LANES)
    word = jnp.where(inside, (1 << 30) + ((place - rank) << 16) + local, 0)
    step = 0
    while (1 << step) < top_count:
        moved = pltpu.roll(word, rows - (1 << step), 0)
        bit = 1 << (16 + step)
        word = jnp.where((moved & bit) != 0, moved, jnp.where((word & bit) != 0, 0, word))
        step += 1
    index = jnp.where(word != 0, word & 0xFFFF, -1)
    return jnp.concatenate(
        [index[layer * top_count : layer * top_count + slab_most] for layer in range(layers)], axis=0
    )


def by_token(kept):
    used, tokens = kept.shape
    folds = LANES // used
    part = iota(kept.shape, 1) // (tokens // folds)
    return jnp.transpose(
        jnp.concatenate([jnp.where(part == f, kept, -1) for f in range(folds)], axis=0), (1, 0)
    )


def inverse_kernel(plan, kept_ref, inverse_ref, rows_ref):
    layers, width, top_count, slab_most = plan
    tokens = kept_ref.shape[1]
    blocks = width // LANES
    words = -(-blocks // WORD_BLOCKS)
    used = layers * slab_most
    part = iota((tokens, LANES), 0) // (tokens * used // LANES)
    unused = (part + 1) % (LANES // used) * used
    for layer in range(layers):
        own = kept_ref[layer * slab_most : (layer + 1) * slab_most, :]
        block = lax.shift_right_arithmetic(own, 7) - layer * stride(width)
        number = iota(own.shape, 0) + (1 + layer * slab_most)
        value = lax.shift_left(number, NUMBER_BITS * (block % WORD_BLOCKS))
        rows_ref[layer, 0] = jnp.bitwise_and(own, LANES - 1)
        for w in range(words):
            rows_ref[layer, 1 + w] = jnp.where((own >= 0) & (block // WORD_BLOCKS == w), value, 0)
        pieces = [[] for w in range(words)]
        for first in range(0, LANES, CHUNK):
            lane = iota((CHUNK, tokens), 0) + first
            totals = [jnp.zeros((CHUNK, tokens), jnp.int32) for w in range(words)]
            for s in range(slab_most):
                match = lane == rows_ref[layer, 0, s : s + 1, :]
                for w in range(words):
                    totals[w] = totals[w] + jnp.where(match, rows_ref[layer, 1 + w, s : s + 1, :], 0)
            for w in range(words):
                pieces[w].append(totals[w])
        for w in range(words):
            word = jnp.transpose(jnp.concatenate(pieces[w], axis=0), (1, 0))
            for b in range(w * WORD_BLOCKS, min((w + 1) * WORD_BLOCKS, blocks)):
                numbers = lax.shift_right_logical(word, NUMBER_BITS * (b % WORD_BLOCKS))
                numbers = jnp.bitwise_and(numbers, LANES - 1)
                lanes = jnp.where(numbers > 0, numbers - 1 + part * used, unused)
                inverse_ref[layer, :, b * LANES : (b + 1) * LANES] = lanes.astype(jnp.int16)


def encode_kernel(
    plan, x_hbm, encoder_hbm, bias_hbm, top_hbm, z_ref, index_ref, kept_ref,
    x_ref, encoder_ref, bias_ref, top_ref, x_layer, sems
):
    layers, width, top_count, slab_most = plan
    copies = [
        pltpu.make_async_copy(source, target, sems.at[i])
        for i, (source, target) in enumerate(
            [(top_hbm, top_ref), (x_hbm, x_ref), (bias_hbm, bias_ref), (encoder_hbm, encoder_ref)]
        )
    ]
    for copy in copies:
        copy.start()
    for copy in copies[:2]:
        copy.wait()
    tokens, depth = x_ref.shape[0], x_ref.shape[2]
    x_rows = x_ref[...].reshape(tokens * layers, depth)
    token, row = iota((tokens, tokens * layers), 0), iota((tokens, tokens * layers), 1)
    for layer in range(layers):
        x_layer[layer] = matmul(flag(row == layers * token + layer), x_rows).astype(BF)
    kept = slot_index(top_ref[...], lax.axis_index("lat"), width, layers, top_count, slab_most)
    kept_ref[...] = kept
    index = by_token(kept).astype(jnp.int16)
    index_ref[...] = index
    for copy in copies[2:]:
        copy.wait()
    with_bias = jnp.where(lax.axis_index("layer") == 0, 1.0, 0.0)
    picked = []
    for layer in range(layers):
        dense = matmul(x_layer[layer], encoder_ref[layer])
        dense = dense + bias_ref[layer : layer + 1, :] * with_bias
        picked.append(gather_slots(dense, index))
    z_ref[...] = fold_slots(join_layers(picked, index, width), layers * slab_most)


def block_places(layers, pair):
    return [(k, 0) if k <= pair else (k - pair - 1, 1) for k in range(layers + 1)]


def decode_kernel(
    plan, pair, parts_ref, inverse_ref, decoder_ref, index_ref,
    act_ref, first_ref, second_ref, first_rounded, second_rounded, index_out
):
    layers, width, top_count, slab_most = plan
    index_out[...] = index_ref[...]
    total = sum_parts(parts_ref, layers * slab_most)
    for layer in range(layers):
        act_ref[layer] = place_slots(total, inverse_ref[layer])
    sums = [None, None]
    for k, (source, slot) in enumerate(block_places(layers, pair)):
        term = matmul(act_ref[source], decoder_ref[k])
        sums[slot] = term if sums[slot] is None else sums[slot] + term
    first_ref[...] = sums[0]
    second_ref[...] = sums[1]
    first_rounded[...] = sums[0].astype(BF)
    second_rounded[...] = sums[1].astype(BF)


def turn_kernel(act_ref, x_ref, targets_ref, decoder_ref, act_t, x_t, targets_out, decoder_t):
    for layer in range(act_ref.shape[0]):
        act_t[layer] = jnp.transpose(act_ref[layer], (1, 0))
        x_t[layer] = jnp.transpose(x_ref[:, layer, :], (1, 0))
    for slot in range(2):
        targets_out[slot] = targets_ref[:, slot, :]
    for k in range(decoder_ref.shape[0]):
        decoder_t[k] = jnp.transpose(decoder_ref[k], (1, 0))


def residue_kernel(
    plan, pair, mine_a, mine_b, theirs_a, theirs_b, dec_bias_ref, targets_ref, index_ref, decoder_t,
    act_t, z_ref, residue, head_ref
):
    layers, width, top_count, slab_most = plan
    for slot, (mine, theirs) in enumerate([(mine_a, theirs_a), (mine_b, theirs_b)]):
        rebuilt = mine[...] + theirs[...].astype(F32)
        rebuilt = rebuilt + dec_bias_ref[slot : slot + 1, :]
        residue[slot] = (rebuilt - targets_ref[slot].astype(F32)).astype(BF)
    places = block_places(layers, pair)
    index = index_ref[...]
    picked = []
    for layer in range(layers):
        own = [(k, slot) for k, (source, slot) in enumerate(places) if source == layer]
        if own:
            left = jnp.concatenate([residue[slot] for k, slot in own], axis=1)
            right = jnp.concatenate([decoder_t[k] for k, slot in own], axis=0)
            picked.append(gather_slots(matmul(left, right), index))
        else:
            picked.append(jnp.zeros(index.shape, BF))
    z_ref[...] = fold_slots(join_layers(picked, index, width), layers * slab_most)
    head_ref[...] = matmul(act_t[places[0][0]], residue[places[0][1]])


def grads_kernel(
    plan, pair, parts_ref, inverse_ref, x_t, act_t, residue_ref, head_ref,
    decoder_hbm, encoder_hbm, bias_hbm, values, decoder_grad, encoder_grad, bias, sems
):
    layers, width, top_count, slab_most = plan
    tokens = x_t.shape[2]
    part = width // PARTS
    copies = []

    def send(source, target):
        copies.append(pltpu.make_async_copy(source, target, sems.at[len(copies)]))
        copies[-1].start()

    send(head_ref, decoder_hbm.at[0])
    values[...] = sum_parts(parts_ref, layers * slab_most)
    ones = jnp.ones((8, tokens), BF)
    for layer in range(layers):
        for i in range(PARTS):
            at = (layer, slice(None), pl.ds(i * part, part))
            dense = place_slots(values[...], inverse_ref[at])
            encoder_grad[at] = matmul(x_t[layer], dense)
            send(encoder_grad.at[at], encoder_hbm.at[at])
            bias[layer : layer + 1, i * part : (i + 1) * part] = matmul(ones, dense)[:1]
    for k, (source, slot) in list(enumerate(block_places(layers, pair)))[1:]:
        for i in range(PARTS):
            rows = pl.ds(i * part, part)
            decoder_grad[k - 1, rows] = matmul(act_t[source, rows], residue_ref[slot])
            send(decoder_grad.at[k - 1, rows], decoder_hbm.at[k, rows])
    send(bias, bias_hbm)
    for copy in copies:
        copy.wait()


VMEM = pl.BlockSpec(memory_space=pltpu.VMEM)
HBM = pl.BlockSpec(memory_space=pltpu.HBM)
MIB = 1024 * 1024


def call(kernel, ins, outs, scratch, *args, cost=None, room=24):
    args = [
        pltpu.with_memory_space_constraint(arg, pltpu.HBM) if spec is HBM else arg
        for spec, arg in zip(ins, args, strict=True)
    ]
    return pl.pallas_call(
        kernel,
        out_shape=tuple(
            (pltpu.HBM if spec is HBM else pltpu.VMEM)(shape, dtype) for shape, dtype, spec in outs
        ),
        in_specs=ins,
        out_specs=tuple(spec for _, _, spec in outs),
        scratch_shapes=scratch,
        cost_estimate=cost,
        compiler_params=pltpu.CompilerParams(vmem_limit_bytes=room * MIB),
    )(*args)


def share(value, axis):
    copies = jnp.broadcast_to(value[None], (lax.axis_size(axis),) + value.shape)
    return lax.all_to_all(copies, axis, 0, 0, tiled=True)


def by_pair(pairs, build, *args):
    branches = [functools.partial(build, pair) for pair in range(pairs)]
    if pairs == 1:
        return branches[0](*args)
    return lax.switch(lax.axis_index("layer") // FEAT_SPLIT, branches, *args)


def across(value, axis, step):
    pairs = [(i, i ^ step) for i in range(lax.axis_size(axis))]
    return lax.ppermute(value, axis, pairs)


def body(inputs, encoder, enc_bias, decoder, dec_bias, targets, top_index):
    tokens, layers, top_count = top_index.shape
    depth, width = encoder.shape[1:]
    feat = decoder.shape[3]
    slabs = lax.axis_size("lat")
    slab_most = 2 * top_count // slabs
    packed = tokens * layers * slab_most // LANES
    pairs = lax.axis_size("layer") // FEAT_SPLIT
    plan = (layers, width, top_count, slab_most)
    top = jnp.transpose(top_index, (1, 2, 0)).reshape(layers * top_count, tokens)
    dma = pltpu.SemaphoreType.DMA
    i16, i32 = jnp.int16, jnp.int32
    z, index, kept = call(
        functools.partial(encode_kernel, plan),
        [HBM] * 4,
        [
            ((packed, LANES), BF, VMEM),
            ((tokens, LANES), i16, VMEM),
            ((layers * slab_most, tokens), i32, VMEM),
        ],
        [
            pltpu.VMEM(inputs.shape, BF),
            pltpu.VMEM(encoder.shape, BF),
            pltpu.VMEM(enc_bias.shape, F32),
            pltpu.VMEM(top.shape, i32),
            pltpu.VMEM((layers, tokens, depth), BF),
            dma((4,)),
        ],
        inputs, encoder, enc_bias, top,
    )
    parts = share(z, "layer")
    (inverse,) = call(
        functools.partial(inverse_kernel, plan),
        [VMEM],
        [((layers, tokens, width), i16, VMEM)],
        [pltpu.VMEM((layers, 1 - (-width // (LANES * WORD_BLOCKS)), slab_most, tokens), i32)],
        kept,
        cost=pl.CostEstimate(flops=10**8, bytes_accessed=10**6, transcendentals=0),
    )

    def decode(pair, *args):
        return call(
            functools.partial(decode_kernel, plan, pair),
            [VMEM] * 4,
            [
                ((layers, tokens, width), BF, VMEM),
                ((tokens, feat), F32, VMEM),
                ((tokens, feat), F32, VMEM),
                ((tokens, feat), BF, VMEM),
                ((tokens, feat), BF, VMEM),
                ((tokens, LANES), i16, VMEM),
            ],
            [],
            *args,
        )

    act, mine_a, mine_b, sent_a, sent_b, index = by_pair(
        pairs, decode, parts, inverse, decoder[0], index
    )
    def turn(act):
        return call(
            turn_kernel,
            [VMEM] * 4,
            [
                ((layers, width, tokens), BF, VMEM),
                ((layers, depth, tokens), BF, VMEM),
                ((2, tokens, feat), BF, VMEM),
                ((layers + 1, feat, width), BF, VMEM),
            ],
            [],
            act, inputs, targets[0], decoder[0],
            cost=pl.CostEstimate(flops=10**8, bytes_accessed=10**7, transcendentals=0),
        )

    steps = [1 << i | 1 for i in range(slabs.bit_length() - 1)]
    turned = None
    for i in range(len(steps)):
        theirs_a = across(sent_a, "lat", 1 << i)
        theirs_b = across(sent_b, "lat", steps[-1 - i])
        if i + 1 < len(steps):
            mine_a = mine_a + theirs_a.astype(F32)
            sent_a = mine_a.astype(BF)
            if i + 2 == len(steps):
                sent_a, act = lax.optimization_barrier((sent_a, act))
                turned = turn(act)
            mine_b = mine_b + theirs_b.astype(F32)
            sent_b = mine_b.astype(BF)
            if turned is not None:
                sent_b, turned = lax.optimization_barrier((sent_b, turned))
    act_t, x_t, targets_by_slot, decoder_t = turn(act) if turned is None else turned

    def residues(pair, *args):
        return call(
            functools.partial(residue_kernel, plan, pair),
            [VMEM] * 9,
            [
                ((packed, LANES), BF, VMEM),
                ((2, tokens, feat), BF, VMEM),
                ((width, feat), F32, VMEM),
            ],
            [],
            *args,
        )

    z, residue, head = by_pair(
        pairs, residues, mine_a, mine_b, theirs_a, theirs_b, dec_bias[0], targets_by_slot, index, decoder_t, act_t
    )
    parts = share(z, "layer")

    def grads(pair, *args):
        return call(
            functools.partial(grads_kernel, plan, pair),
            [VMEM] * 6,
            [
                ((layers + 1, width, feat), F32, HBM),
                (encoder.shape, F32, HBM),
                (enc_bias.shape, F32, HBM),
            ],
            [
                pltpu.VMEM((tokens, LANES), BF),
                pltpu.VMEM((layers, width, feat), F32),
                pltpu.VMEM(encoder.shape, F32),
                pltpu.VMEM(enc_bias.shape, F32),
                dma((PARTS * 2 * layers + 2,)),
            ],
            *args,
        )

    decoder_grad, encoder_grad, bias_grad = by_pair(
        pairs, grads, parts, inverse, x_t, act_t, residue, head
    )
    return decoder_grad[None], encoder_grad, bias_grad


def solution(mesh):
    return jax.shard_map(
        body,
        mesh=mesh,
        in_specs=(
            P(None, None, "layer"),
            P(None, "layer", "lat"),
            P(None, "lat"),
            P("layer", None, "lat", None),
            P("layer", None, None),
            P("layer", None, None, None),
            P(),
        ),
        out_specs=(P("layer", None, "lat", None), P(None, "layer", "lat"), P(None, "lat")),
        check_vma=False,
    )
```
